32 devices in a mesh: hour: 2 (over x), rcpt: 16 (over z, y, core).
Axes of the slice: x: 2, y: 2, z: 4, core: 2. Of those that a mesh axis runs over, the one named last changes fastest.
Arguments:
- flux: float32 [192, 4096], P('hour', 'rcpt'), may hold values from -6 to 6
- footprint: bfloat16 [4096, 8, 4096], P(('hour', 'rcpt')), may hold values from -0.0625 to 0.0625
- tile_mask: int32 [256, 8, 32], P(('hour', 'rcpt')), may hold values 0 or 1
- rec_hour: int32 [4096], P(('hour', 'rcpt')), may hold values from 0 to 95
- observed: float32 [4096], P(('hour', 'rcpt')), may hold values from -6 to 6
- obs_weight: float32 [4096], P(('hour', 'rcpt')), may hold values from 0.2 to 5
- site_count: int32 [32], P(('hour', 'rcpt')), may hold values from 1 to 128, 2560 in all
Outputs:
- gradient: float32 [192, 4096], P('hour', 'rcpt')
- mismatch: float32 [4096], P(('hour', 'rcpt'))
The draws below stay inside these ranges and needn't reach their ends.
Inputs may be any that keep to these rules, and one draw needn't show every extreme that they name: `site_count`: at most 128 live receptors in a shard; some shard has exactly 128.
All inputs are finite; a program needn't handle non-finite values. No bound on the sum of `tile_mask` on one device may be relied on, other than what follows from the above.
Results may differ from the reference program's by a relative error of at most 0.0036.
Values may be sent and summed in bfloat16 or wider, within the bound.
No kernel may reach another device: no remote copies, remote signals or barrier semaphores. Data moves between devices by JAX's collectives and lax.ppermute only.
A program may use at most 64 MiB of HBM per device.

```python
import math
import jax
import jax.numpy as jnp
import numpy as np
from jax import lax

CELLS = 4096
TILE = 128
LAGS = 8
RBLK = 16
HB = 96
R_DEV = 128
SHARDS = 32
RECEPTORS = 4096
HOURS = 192
TILES = 32
N_RCPT = 16


def plant(drawn, own_key, low, high):
    longest = drawn.shape.index(max(drawn.shape))
    spots = []
    for shift in (0, 1):
        where = [jax.random.randint(jax.random.fold_in(own_key, axis), (), 0, length) for axis, length in enumerate(drawn.shape)]
        where[longest] = (where[longest] + shift) % drawn.shape[longest]
        spots.append(tuple(where))
    return drawn.at[spots[0]].set(low).at[spots[1]].set(high)


def strengthened(values, own_key, source, target, parts, factor):
    def block_of(position):
        return (jnp.arange(values.shape[position]) // (values.shape[position] // parts)).reshape((-1,) + (1,) * (values.ndim - 1 - position))

    near = jax.random.permutation(own_key, parts)[block_of(target)]
    other_side = (block_of(target) + parts // 2) % parts
    return jnp.where((block_of(source) == near) | (block_of(source) == other_side), factor * values, values)


def level_of(rng, dims, pieces, low, top_value):
    factor_of = 1.0
    for dim, blocks in pieces:
        draws = jax.random.uniform(jax.random.fold_in(jax.random.fold_in(rng, 6), dim), (blocks,), jnp.float32, low / len(pieces), top_value / len(pieces))
        factor_of = factor_of * jnp.repeat(jnp.exp(draws), dims[dim] // blocks).reshape((-1,) + (1,) * (len(dims) - 1 - dim))
    return factor_of


def profile(count, total, bound, slope):
    weights = [(1 << 20) // math.isqrt(rank ** slope) + 1 for rank in range(2, count + 1)]
    rest, given = total - bound - (count - 1), [1] * (count - 1)
    while rest > 0:
        candidates = [i for i in range(count - 1) if given[i] < bound]
        whole, left = sum([weights[i] for i in candidates]), rest
        for i in candidates:
            extra = min(bound - given[i], max(1, left * weights[i] // whole), rest)
            given[i] = given[i] + extra
            rest = rest - extra
    return np.array([bound] + given)


def uneven(rng, count, total, most, slope):
    if count == 2:
        one = jax.random.randint(rng, (), max(1, total - most), min(most, total - 1) + 1)
        return jnp.stack([one, total - one])
    sizes = jnp.asarray(profile(count, total, most, slope), jnp.int32)
    twos = (count - 1) // 2
    donor, receiver = sizes[1:1 + 2 * twos:2], sizes[2:2 + 2 * twos:2]
    room = jnp.minimum(donor - 1, most - receiver)
    shifted = jax.random.randint(jax.random.fold_in(rng, 1), (twos,), 0, 1 << 20) % (room + 1)
    sizes = sizes.at[1:1 + 2 * twos:2].set(donor - shifted).at[2:2 + 2 * twos:2].set(receiver + shifted)
    return sizes[jax.random.permutation(jax.random.fold_in(rng, 2), count)]


def scatter_about(rng, extent, spread, bound, split=(), held_as=jnp.bfloat16):
    values = spread * jax.random.normal(rng, extent, jnp.float32)
    if split:
        values = values * level_of(rng, extent, split, -0.22, 0.18)
    return jnp.clip(values, -bound, bound).astype(held_as)


def gaussian_with(key, dims, deviation, bound, shards, heavy, held_as=jnp.bfloat16):
    drawn = deviation * jax.random.normal(key, dims, jnp.float32)
    if shards:
        drawn = drawn * level_of(key, dims, shards, -0.22, 0.18)
    return jnp.clip(strengthened(drawn, jax.random.fold_in(key, 3), *heavy), -bound, bound).astype(held_as)


def setup_inputs(seed: int = 0) -> dict:
    splits = jax.random.split(jax.random.key(seed), 8)
    flux = scatter_about(splits[0], (HOURS, CELLS), 1.0, 6.0, ((0, 2), (1, 16)), jnp.float32)
    footprint = gaussian_with(splits[1], (RECEPTORS, LAGS, CELLS), (LAGS * CELLS) ** -0.5, 0.0625, ((0, 32),), (0, 2, 32, 2.75))
    tile_mask = plant((jax.random.randint(splits[2], (RECEPTORS // RBLK, LAGS, TILES), 0, 4) < 3).astype(jnp.int32), jax.random.fold_in(splits[2], 1), 0, 1)
    rec_hour = plant(jax.random.randint(splits[3], (RECEPTORS,), 0, HB), jax.random.fold_in(splits[3], 1), 0, HB - 1).astype(jnp.int32)
    observed = scatter_about(splits[4], (RECEPTORS,), 1.0, 6.0, ((0, 32),), jnp.float32)
    obs_weight = jnp.clip(jnp.exp(math.log(5.0) - 3.218876 * jax.random.uniform(splits[5], (RECEPTORS,), jnp.float32) ** level_of(splits[5], (RECEPTORS,), ((0, 32),), -0.2, 0.2)), 0.2, 5.0)
    site_count = uneven(splits[6], SHARDS, SHARDS * R_DEV * 5 // 8, R_DEV, 2).astype(jnp.int32)
    return dict(flux=flux, footprint=footprint, tile_mask=tile_mask, rec_hour=rec_hour, observed=observed, obs_weight=obs_weight, site_count=site_count)


def reference(flux, footprint, tile_mask, rec_hour, observed, obs_weight, site_count):
    low = flux.astype(jnp.bfloat16)
    padded = jnp.concatenate([jnp.zeros((LAGS - 1, CELLS), jnp.bfloat16), low], axis=0)
    per_shard = R_DEV // RBLK
    lag_index = jnp.arange(LAGS, dtype=jnp.int32)

    def one_shard(total, index):
        start = (index * R_DEV).astype(jnp.int32)
        fblock = lax.dynamic_slice_in_dim(footprint, start, R_DEV, 0)
        mblock = lax.dynamic_slice_in_dim(tile_mask, (index * per_shard).astype(jnp.int32), per_shard, 0)
        expand = jnp.repeat(jnp.repeat(mblock, RBLK, axis=0), TILE, axis=2).astype(jnp.bfloat16)
        masked = fblock * expand
        hours = lax.dynamic_slice_in_dim(rec_hour, start, R_DEV, 0)
        block = (index // N_RCPT).astype(jnp.int32)
        slots = (block * HB + hours[:, None] - lag_index[None, :] + LAGS - 1).astype(jnp.int32)
        picked = padded[slots]
        model = jnp.sum(masked.astype(jnp.float32) * picked.astype(jnp.float32), axis=(1, 2))
        live = (jnp.arange(R_DEV, dtype=jnp.int32) < site_count[index]).astype(jnp.float32)
        obs = lax.dynamic_slice_in_dim(observed, start, R_DEV, 0)
        weight = lax.dynamic_slice_in_dim(obs_weight, start, R_DEV, 0)
        mism = live * weight * (model - obs)
        rounded = lax.optimization_barrier(mism.astype(jnp.bfloat16)).astype(jnp.float32)
        terms = masked.astype(jnp.float32) * rounded[:, None, None]
        total = total.at[slots].add(terms)
        return total, mism

    start_total = jnp.zeros((HOURS + LAGS - 1, CELLS), jnp.float32)
    total, mism = lax.scan(one_shard, start_total, jnp.arange(SHARDS, dtype=jnp.int32))
    return total[LAGS - 1:], mism.reshape(-1)
```

```python
import functools

import jax
import jax.numpy as jnp
from jax import lax
from jax.experimental import pallas as pl
from jax.experimental.pallas import tpu as pltpu
from jax.sharding import PartitionSpec as P

RIM = 8
F32 = jnp.float32
BF16 = jnp.bfloat16
VMEM_LIMIT = 40 * 1024 * 1024


def swap(block, bit):
    devices = range(lax.axis_size("rcpt"))
    return lax.ppermute(block, "rcpt", [(i, i ^ bit) for i in devices])


def turn(block, distance):
    size = lax.axis_size("hour")
    return lax.ppermute(block, "hour", [(i, (i + distance) % size) for i in range(size)])


def expander(rows, lags, dtype):
    shape = (rows, rows * lags)
    row = lax.broadcasted_iota(jnp.int32, shape, 0)
    column = lax.broadcasted_iota(jnp.int32, shape, 1)
    first = row * lags
    return ((column >= first) & (column < first + lags)).astype(dtype)


def prepare_kernel(me_ref, foot_ref, mask_ref, hour_ref, masked_ref, select_ref):
    step = pl.program_id(0)
    blocks, lags, tiles = mask_ref.shape
    depth, own = foot_ref.shape
    width = select_ref.shape[0]
    rows = depth // lags
    group = 2 * lags
    tile = own * pl.num_programs(0) // tiles

    @pl.when(step == 0)
    def _():
        hours = jnp.broadcast_to(hour_ref[...].astype(F32), (8, rows)).astype(BF16)
        spread = jnp.dot(hours, expander(rows, lags, BF16), preferred_element_type=F32)
        column = lax.broadcasted_iota(jnp.int32, (1, depth), 1)
        slot = spread[:1].astype(jnp.int32) - lax.rem(column, lags) + RIM
        line = lax.broadcasted_iota(jnp.int32, (width, depth), 0)
        select_ref[...] = (line == slot).astype(F32).astype(BF16)

    device = me_ref[0] ^ step
    mask = mask_ref[...].astype(F32)
    twice = jnp.broadcast_to(mask[:, None], (blocks, 2, lags, tiles)).reshape(blocks * group, tiles)
    per = own // tile
    shape = (tiles, own)
    wanted = device * per + lax.broadcasted_iota(jnp.int32, shape, 1) // tile
    widen = (lax.broadcasted_iota(jnp.int32, shape, 0) == wanted).astype(F32).astype(BF16)
    wide = jnp.dot(twice.astype(BF16), widen, preferred_element_type=F32).astype(BF16)
    part = depth // blocks
    for b in range(blocks):
        line = wide[b * group : (b + 1) * group]
        for j in range(part // group):
            at = pl.ds(b * part + j * group, group)
            masked_ref[0, at, :] = foot_ref[at, :] * line


def prepare(me, foot, mask, hour, devices, width):
    depth, cells = foot.shape
    own = cells // devices
    grid_spec = pltpu.PrefetchScalarGridSpec(
        num_scalar_prefetch=1,
        grid=(devices,),
        in_specs=[
            pl.BlockSpec((depth, own), lambda k, me: (0, me[0] ^ k)),
            pl.BlockSpec(mask.shape, lambda k, me: (0, 0, 0)),
            pl.BlockSpec(hour.shape, lambda k, me: (0, 0)),
        ],
        out_specs=[
            pl.BlockSpec((1, depth, own), lambda k, me: (k, 0, 0)),
            pl.BlockSpec((width, depth), lambda k, me: (0, 0)),
        ],
    )
    return pl.pallas_call(
        prepare_kernel,
        grid_spec=grid_spec,
        out_shape=[
            jax.ShapeDtypeStruct((devices, depth, own), BF16),
            jax.ShapeDtypeStruct((width, depth), BF16),
        ],
        cost_estimate=pl.CostEstimate(
            flops=depth * cells, bytes_accessed=4 * depth * cells, transcendentals=0
        ),
        name="prepare",
    )(me, foot, mask, hour)


def adjoint_kernel(devices, lags, *refs):
    chunks = refs[:devices]
    masked_ref, select_ref, obs_ref, weight_ref, count_ref = refs[devices : devices + 5]
    mism_ref, own_ref, other_ref = refs[devices + 5 : devices + 8]
    score_ref, spread_ref = refs[devices + 8 :]
    width, depth = score_ref.shape
    rows = depth // lags
    for k in range(devices):
        dims = (((1,), (1,)), ((), ()))
        term = lax.dot_general(chunks[k][...], masked_ref[k], dims, preferred_element_type=F32)
        if k == 0:
            score_ref[...] = term
        else:
            score_ref[...] += term
    chosen = score_ref[...] * select_ref[...].astype(F32)
    line = jnp.sum(chosen, axis=0, keepdims=True)
    belongs = expander(rows, lags, F32)
    model = lax.dot_general(
        jnp.broadcast_to(line, (8, depth)),
        belongs,
        (((1,), (1,)), ((), ())),
        precision=lax.Precision.HIGHEST,
        preferred_element_type=F32,
    )[:1]
    live = (lax.broadcasted_iota(jnp.int32, (1, rows), 1) < count_ref[0]).astype(F32)
    mism = live * weight_ref[...] * (model - obs_ref[...])
    mism_ref[...] = mism
    weighted = jnp.broadcast_to(mism, (8, rows)).astype(BF16)
    wide = jnp.dot(weighted, belongs.astype(BF16), preferred_element_type=F32)[:1]
    spread_ref[...] = (select_ref[...].astype(F32) * wide).astype(BF16)
    for k in range(1, devices, 2):
        part = jnp.dot(spread_ref[...], masked_ref[k], preferred_element_type=F32)
        other_ref[k // 2] = part.astype(BF16)
    for k in range(0, devices, 2):
        own_ref[k // 2] = jnp.dot(spread_ref[...], masked_ref[k], preferred_element_type=F32)


def adjoint(chunks, masked, select, obs, weight, count, lags):
    devices, depth, own = masked.shape
    width = select.shape[0]
    vmem = pl.BlockSpec(memory_space=pltpu.VMEM)
    half = devices // 2
    return pl.pallas_call(
        functools.partial(adjoint_kernel, devices, lags),
        in_specs=[vmem] * (devices + 4) + [pl.BlockSpec(memory_space=pltpu.SMEM)],
        out_specs=[vmem] * 3,
        out_shape=[
            jax.ShapeDtypeStruct(obs.shape, F32),
            jax.ShapeDtypeStruct((half, width, own), F32),
            jax.ShapeDtypeStruct((half, width, own), BF16),
        ],
        scratch_shapes=[pltpu.VMEM((width, depth), F32), pltpu.VMEM((width, depth), BF16)],
        compiler_params=pltpu.CompilerParams(vmem_limit_bytes=VMEM_LIMIT),
        name="adjoint",
    )(*chunks, masked, select, obs, weight, count)


def join_kernel(own_ref, came_ref, *outs):
    for k, out in enumerate(outs):
        total = own_ref[k] + came_ref[k].astype(F32)
        out[...] = total.astype(out.dtype)


def join(own, came, kept):
    half, width, columns = own.shape
    vmem = pl.BlockSpec(memory_space=pltpu.VMEM)
    return pl.pallas_call(
        join_kernel,
        in_specs=[vmem] * 2,
        out_specs=[vmem] * half,
        out_shape=[
            jax.ShapeDtypeStruct((width, columns), F32 if k in kept else BF16) for k in range(half)
        ],
        name="join",
    )(own, came)


def per_device(flux, footprint, tile_mask, rec_hour, observed, obs_weight, site_count):
    hours, own = flux.shape
    rows, lags, cells = footprint.shape
    devices = cells // own
    far = devices // 2
    near = range(2, far, 2)
    width = hours + RIM
    here = lax.axis_index("hour")
    last = lax.axis_size("hour") - 1
    me = lax.axis_index("rcpt").astype(jnp.int32).reshape(1)

    low = flux.astype(BF16)
    rim = turn(low[hours - RIM :], 1)
    rim = jnp.where(here > 0, rim, jnp.zeros_like(rim))
    window = jnp.concatenate([rim, low], axis=0)

    masked, select = prepare(
        me, footprint.reshape(rows * lags, cells), tile_mask, rec_hour.reshape(1, rows), devices, width
    )

    got = {0: window, far: swap(window, far)}
    for k in near:
        got[k] = swap(window, k)
    for k in near:
        got[far ^ k] = swap(got[far], k)
    for k in range(0, devices, 2):
        got[k ^ 1] = swap(got[k], 1)

    mism, mine, other = adjoint(
        [got[k] for k in range(devices)],
        masked,
        select,
        observed.reshape(1, rows),
        obs_weight.reshape(1, rows),
        site_count,
        lags,
    )
    sums = join(mine, swap(other, 1), (0, far // 2))
    sums = {2 * i: s for i, s in enumerate(sums)}
    across = [swap(sums[far ^ k], k) for k in near]
    close = [swap(sums[k], k) for k in near]
    relay = sums[far]
    for piece in across:
        relay = relay + piece.astype(F32)
    total = sums[0]
    for piece in close + [swap(relay.astype(BF16), far)]:
        total = total + piece.astype(F32)
    back = turn(total[:RIM], -1)
    back = jnp.where(here < last, back, jnp.zeros_like(back))
    gradient = total[RIM:] + jnp.pad(back, ((hours - RIM, 0), (0, 0)))
    return (gradient, mism.reshape(rows))


def solution(mesh):
    placed = (
        P("hour", "rcpt"),
        P(("hour", "rcpt"), None, None),
        P(("hour", "rcpt"), None, None),
        P(("hour", "rcpt")),
        P(("hour", "rcpt")),
        P(("hour", "rcpt")),
        P(("hour", "rcpt")),
    )
    return jax.shard_map(
        per_device,
        mesh=mesh,
        in_specs=placed,
        out_specs=(P("hour", "rcpt"), P(("hour", "rcpt"))),
        check_vma=False,
    )
```

```python
import functools

import jax
import jax.numpy as jnp
from jax import lax
from jax.experimental import pallas as pl
from jax.experimental.pallas import tpu as pltpu
from jax.sharding import PartitionSpec as P

RIM = 8
PAIR = 2 * RIM
F32 = jnp.float32
BF16 = jnp.bfloat16
VMEM_LIMIT = 44 * 1024 * 1024
SMALL_LIMIT = 8 * 1024 * 1024
BUSY = 10**10


def swap(block, bit):
    devices = range(lax.axis_size("rcpt"))
    return lax.ppermute(block, "rcpt", [(i, i ^ bit) for i in devices])


def turn(block, distance):
    size = lax.axis_size("hour")
    return lax.ppermute(block, "hour", [(i, (i + distance) % size) for i in range(size)])


def expander(rows, lags, dtype):
    shape = (rows, rows * lags)
    row = lax.broadcasted_iota(jnp.int32, shape, 0)
    column = lax.broadcasted_iota(jnp.int32, shape, 1)
    first = row * lags
    return ((column >= first) & (column < first + lags)).astype(dtype)


def call(kernel, outs, operands, spaces, scratch=(), limit=SMALL_LIMIT, flops=0, moved=0, name=None):
    where = {"v": pltpu.VMEM, "s": pltpu.SMEM, "a": pl.ANY}
    vmem = pl.BlockSpec(memory_space=pltpu.VMEM)
    return pl.pallas_call(
        kernel,
        in_specs=[pl.BlockSpec(memory_space=where[c]) for c in spaces],
        out_specs=[vmem] * len(outs),
        out_shape=[jax.ShapeDtypeStruct(shape, dtype) for shape, dtype in outs],
        scratch_shapes=scratch,
        compiler_params=pltpu.CompilerParams(vmem_limit_bytes=limit),
        cost_estimate=pl.CostEstimate(flops=flops, bytes_accessed=moved, transcendentals=0),
        name=name,
    )(*operands)


def prepare_kernel(devices, start, foot_hbm, mask_ref, after_ref, masked_ref, foot_ref, sems):
    del after_ref
    me = lax.axis_index("rcpt")
    blocks, lags, tiles = mask_ref.shape
    depth, cells = foot_ref.shape
    own = cells // devices
    tile = cells // tiles
    group = 2 * lags
    part = foot_hbm.shape[0] // blocks
    used = depth // part
    first = start * used
    copies = []
    for b in range(used):
        source = foot_hbm.at[pl.ds((first + b) * part, part)]
        copies.append(pltpu.make_async_copy(source, foot_ref.at[pl.ds(b * part, part)], sems.at[b]))
    for copy in copies:
        copy.start()
    mask = mask_ref[first : first + used].astype(F32)
    twice = jnp.broadcast_to(mask[:, None], (used, 2, lags, tiles)).reshape(used * group, tiles)
    wide = jnp.dot(twice.astype(BF16), expander(tiles, tile, BF16), preferred_element_type=F32)
    wide = wide.astype(BF16)
    for b in range(used):
        copies[b].wait()
        for d in range(devices):
            cut = slice(d * own, (d + 1) * own)
            keep = wide[b * group : (b + 1) * group, cut]
            for j in range(part // group):
                at = pl.ds(b * part + j * group, group)
                masked_ref[me ^ d, at, :] = foot_ref[at, cut] * keep


def prepare(foot, mask, after, devices, start):
    depth, cells = foot.shape
    depth //= 2
    blocks = mask.shape[0] // 2
    return call(
        functools.partial(prepare_kernel, devices, start),
        [((devices, depth, cells // devices), BF16)],
        [foot, mask, after],
        "ava",
        [pltpu.VMEM((depth, cells), BF16), pltpu.SemaphoreType.DMA((blocks,))],
        limit=VMEM_LIMIT,
        flops=BUSY,
        moved=4 * depth * cells,
        name="prepare",
    )[0]


def choose_kernel(lags, hours, hour_ref, obs_ref, weight_ref, count_ref, after_ref, select_ref, line_ref):
    del after_ref
    rows = hour_ref.shape[1]
    times = jnp.broadcast_to(hour_ref[...].astype(F32), (8, rows)).astype(BF16)
    spread = jnp.dot(times, expander(rows, lags, BF16), preferred_element_type=F32)
    column = lax.broadcasted_iota(jnp.int32, (1, rows * lags), 1)
    hour = spread[:1].astype(jnp.int32) - lax.rem(column, lags)
    slot = jnp.where(hour >= 0, hour, hour + (hours + RIM))
    wanted = lax.broadcasted_iota(jnp.int32, select_ref.shape, 0)
    select_ref[...] = (wanted == slot).astype(F32)
    live = (lax.broadcasted_iota(jnp.int32, (1, rows), 1) < count_ref[0]).astype(F32)
    line_ref[0:1] = live * weight_ref[...]
    line_ref[1:2] = obs_ref[...]


def choose(hour, obs, weight, count, after, lags, hours):
    rows = hour.shape[1]
    return call(
        functools.partial(choose_kernel, lags, hours),
        [((hours + PAIR, rows * lags), F32), ((8, rows), F32)],
        [hour, obs, weight, count, after],
        "vvvsa",
        flops=BUSY,
        name="choose",
    )


def tails_kernel(low_ref, far_ref, after_ref, out_ref):
    del after_ref
    hours = low_ref.shape[0]
    ends = [ref[hours - PAIR :].astype(F32)[RIM:] for ref in (low_ref, far_ref)]
    out_ref[...] = jnp.concatenate(ends, axis=0).astype(BF16)


def tails(low, far_low, after):
    outs = [((PAIR, low.shape[1]), BF16)]
    return call(tails_kernel, outs, [low, far_low, after], "vva", name="tails")[0]


def window_kernel(low_ref, far_ref, rims_ref, after_ref, out_ref):
    del after_ref
    hours = low_ref.shape[0]
    inside = (lax.axis_index("hour") > 0).astype(F32)
    out_ref[:hours] = low_ref[...]
    out_ref[hours : 2 * hours] = far_ref[...]
    out_ref[2 * hours :] = (rims_ref[...].astype(F32) * inside).astype(BF16)


def window(low, far_low, rims, after):
    hours, columns = low.shape
    outs = [((2 * hours + PAIR, columns), BF16)]
    return call(window_kernel, outs, [low, far_low, rims, after], "vvva", name="window")[0]


def pack_kernel(*refs):
    *parts, _, out_ref = refs
    height = parts[0].shape[0]
    for i, part in enumerate(parts):
        out_ref[i * height : (i + 1) * height] = part[...]


def pack(parts, after):
    height, columns = parts[0].shape
    outs = [((len(parts) * height, columns), BF16)]
    operands = [*parts, after]
    return call(pack_kernel, outs, operands, "v" * len(operands), name="pack")[0]


def add_scores(windows, masked_refs, start, score_ref, window_ref):
    hours = window_ref.shape[0] - PAIR
    half = masked_refs[0].shape[0] // 2
    depth = masked_refs[0].shape[1]
    for i, read in enumerate(windows):
        rims = read(slice(2 * hours, 2 * hours + PAIR)).astype(F32)
        gap = jnp.zeros_like(rims[:RIM])
        for j in range(2):
            window_ref[:hours] = read(slice(j * hours, (j + 1) * hours))
            rim = rims[j * RIM : (j + 1) * RIM]
            window_ref[hours:] = jnp.concatenate([rim, gap], axis=0).astype(BF16)
            k = (j * half + 2 * i) ^ start
            dims = (((1,), (1,)), ((), ()))
            for n, masked_ref in enumerate(masked_refs):
                at = slice(n * depth, (n + 1) * depth)
                term = lax.dot_general(
                    window_ref[...], masked_ref[k], dims, preferred_element_type=F32
                )
                if start == 0 and i == 0 and j == 0:
                    score_ref[:, at] = term
                else:
                    score_ref[:, at] += term


def readers(first_ref, rest_ref):
    height = first_ref.shape[0]

    def read(i, rows):
        if i == 0:
            return first_ref[rows]
        return rest_ref[(i - 1) * height + rows.start : (i - 1) * height + rows.stop]

    count = 1 + rest_ref.shape[0] // height
    return [functools.partial(read, i) for i in range(count)]


def score_kernel(first_ref, rest_ref, top_ref, low_ref, score_ref, window_ref):
    add_scores(readers(first_ref, rest_ref), (top_ref, low_ref), 0, score_ref, window_ref)


def score(first, rest, masked):
    devices, depth, own = masked[0].shape
    depth *= 2
    width = first.shape[0] // 2 - RIM + PAIR
    return call(
        score_kernel,
        [((width, depth), F32)],
        [first, rest, *masked],
        "vvvv",
        [pltpu.VMEM((width, own), BF16)],
        flops=width * depth * own * devices,
        moved=depth * own * devices,
        name="score",
    )[0]


def terms(spread_ref, masked_refs, k):
    depth = masked_refs[0].shape[1]
    total = None
    for n, masked_ref in enumerate(masked_refs):
        at = slice(n * depth, (n + 1) * depth)
        term = jnp.dot(spread_ref[:, at], masked_ref[k], preferred_element_type=F32)
        total = term if total is None else total + term
    return total


def adjoint_kernel(
    first_ref, rest_ref, top_ref, low_ref, begun_ref, select_ref, line_ref,
    mism_ref, spread_ref, other_ref, score_ref, window_ref,
):
    depth = score_ref.shape[1]
    rows = mism_ref.shape[1]
    lags = depth // rows
    score_ref[...] = begun_ref[...]
    add_scores(readers(first_ref, rest_ref), (top_ref, low_ref), 1, score_ref, window_ref)
    line = jnp.sum(score_ref[...] * select_ref[...], axis=0, keepdims=True)
    belongs = expander(rows, lags, F32)
    model = lax.dot_general(
        jnp.broadcast_to(line, (8, depth)),
        belongs,
        (((1,), (1,)), ((), ())),
        precision=lax.Precision.HIGHEST,
        preferred_element_type=F32,
    )[:1]
    mism = line_ref[0:1] * (model - line_ref[1:2])
    mism_ref[...] = mism
    weighted = jnp.broadcast_to(mism, (8, rows)).astype(BF16)
    wide = jnp.dot(weighted, belongs.astype(BF16), preferred_element_type=F32)[:1]
    spread_ref[...] = (select_ref[...] * wide).astype(BF16)
    for k in range(top_ref.shape[0] // 2):
        other_ref[k] = terms(spread_ref, (top_ref, low_ref), 2 * k + 1).astype(BF16)


def adjoint(first, rest, masked, begun, select, lines):
    devices, depth, own = masked[0].shape
    depth *= 2
    width = begun.shape[0]
    return call(
        adjoint_kernel,
        [
            ((1, lines.shape[1]), F32),
            ((width, depth), BF16),
            ((devices // 2, width, own), BF16),
        ],
        [first, rest, *masked, begun, select, lines],
        "v" * 7,
        [pltpu.VMEM((width, depth), F32), pltpu.VMEM((width, own), BF16)],
        flops=2 * width * depth * own * devices,
        moved=depth * own * devices,
        name="adjoint",
    )


def mine_kernel(spread_ref, top_ref, low_ref, own_ref):
    for k in range(top_ref.shape[0] // 2):
        own_ref[k] = terms(spread_ref, (top_ref, low_ref), 2 * k)


def mine_part(spread, masked):
    devices, depth, own = masked[0].shape
    depth *= 2
    width = spread.shape[0]
    return call(
        mine_kernel,
        [((devices // 2, width, own), F32)],
        [spread, *masked],
        "vvv",
        flops=width * depth * own * devices,
        moved=depth * own * devices,
        name="mine",
    )[0]


def join_kernel(own_ref, came_ref, main_ref, rims_ref):
    half, width, _ = own_ref.shape
    hours = width - PAIR
    for i in range(half // 2):
        edges = []
        for j in range(2):
            k = i + j * (half // 2)
            total = own_ref[k] + came_ref[k].astype(F32)
            main_ref[i, j * hours : (j + 1) * hours] = total[:hours]
            edges.append(total[hours : hours + RIM])
        rims_ref[i * PAIR : (i + 1) * PAIR] = jnp.concatenate(edges, axis=0).astype(BF16)


def join(own, came):
    half, width, columns = own.shape
    outs = [
        ((half // 2, 2 * (width - PAIR), columns), F32),
        ((half // 2 * PAIR, columns), BF16),
    ]
    return call(join_kernel, outs, [own, came], "vv", name="join")


def diagonal_kernel(main_ref, after_ref, out_ref):
    del after_ref
    out_ref[...] = main_ref[main_ref.shape[0] - 1].astype(BF16)


def diagonal(main, after):
    outs = [(main.shape[1:], BF16)]
    return call(diagonal_kernel, outs, [main, after], "vv", flops=BUSY, name="diagonal")[0]


def with_rims(both, rims):
    hours = both.shape[0] // 2
    pieces = []
    for j in range(2):
        at = (j + 1) * hours - RIM
        pieces.append(both[j * hours : at])
        pieces.append(both[at : at + RIM] + rims[j * RIM : (j + 1) * RIM])
    return jnp.concatenate(pieces, axis=0)


def shares_kernel(main_ref, rims_ref, first_ref, edge_ref, *outs):
    inside = (lax.axis_index("hour") < lax.axis_size("hour") - 1).astype(F32)
    for i in range(main_ref.shape[0]):
        rims = rims_ref[i * PAIR : (i + 1) * PAIR].astype(F32) * inside
        if i == 0:
            first_ref[...] = with_rims(main_ref[i], rims)
        elif i == main_ref.shape[0] - 1:
            edge_ref[...] = rims.astype(BF16)
        else:
            outs[i - 1][...] = with_rims(main_ref[i], rims).astype(BF16)


def shares(main, rims):
    count, both, columns = main.shape
    outs = [((both, columns), F32), ((PAIR, columns), BF16)]
    outs += [((both, columns), BF16)] * (count - 2)
    return call(shares_kernel, outs, [main, rims], "vv", name="shares")


def sums_kernel(first_ref, edge_ref, *refs):
    *arrived, total_ref, relay_ref = refs
    hours = total_ref.shape[0]
    total = first_ref[...]
    for piece in arrived:
        total += piece[...].astype(F32)
    total = with_rims(total, edge_ref[...].astype(F32))
    total_ref[...] = total[:hours]
    relay_ref[...] = total[hours:].astype(BF16)


def sums(first, edge, arrived):
    both, columns = first.shape
    main = (both // 2, columns)
    operands = [first, edge, *arrived]
    return call(sums_kernel, [(main, F32), (main, BF16)], operands, "v" * len(operands), name="sums")


def per_device(flux, footprint, tile_mask, rec_hour, observed, obs_weight, site_count):
    hours, own = flux.shape
    rows, lags, cells = footprint.shape
    devices = cells // own
    far = devices // 2
    near = range(2, far - 2, 2)
    diag = far - 2

    low = flux.astype(BF16)
    far_low = swap(low, far)
    foot = footprint.reshape(rows * lags, cells)
    top = prepare(foot, tile_mask, low, devices, 0)
    ends = tails(low, far_low, top)
    bottom = prepare(foot, tile_mask, ends, devices, 1)
    first = window(low, far_low, turn(ends, 1), bottom)
    parts = [swap(first, k) for k in range(2, far, 2)]
    other_first = swap(first, 1)
    select, lines = choose(
        rec_hour.reshape(1, rows),
        observed.reshape(1, rows),
        obs_weight.reshape(1, rows),
        site_count,
        first,
        lags,
        hours,
    )
    rest = pack(parts, lines)
    masked = (top, bottom)
    begun = score(first, rest, masked)
    mism, spread, other = adjoint(other_first, swap(rest, 1), masked, begun, select, lines)

    main, rims = join(mine_part(spread, masked), swap(other, 1))
    back = turn(rims, -1)
    diag_main = swap(diagonal(main, rims), diag)
    first, edge, *outward = shares(main, back)
    arrived = [swap(part, k) for part, k in zip(outward, near)]
    edge = swap(edge, diag)
    total, relay = sums(first, edge, [diag_main, *arrived])
    gradient = total + swap(relay, far).astype(F32)
    return (gradient, mism.reshape(rows))


def solution(mesh):
    placed = (
        P("hour", "rcpt"),
        P(("hour", "rcpt"), None, None),
        P(("hour", "rcpt"), None, None),
        P(("hour", "rcpt")),
        P(("hour", "rcpt")),
        P(("hour", "rcpt")),
        P(("hour", "rcpt")),
    )
    return jax.shard_map(
        per_device,
        mesh=mesh,
        in_specs=placed,
        out_specs=(P("hour", "rcpt"), P(("hour", "rcpt"))),
        check_vma=False,
    )
```

```python
import functools

import jax
import jax.numpy as jnp
from jax import lax
from jax.experimental import pallas as pl
from jax.experimental.pallas import tpu as pltpu
from jax.sharding import PartitionSpec as P

RIM = 8
PAIR = 2 * RIM
F32 = jnp.float32
BF16 = jnp.bfloat16
VMEM_LIMIT = 44 * 1024 * 1024
SMALL_LIMIT = 8 * 1024 * 1024
BUSY = 10**10


def swap(block, bit):
    devices = range(lax.axis_size("rcpt"))
    return lax.ppermute(block, "rcpt", [(i, i ^ bit) for i in devices])


def turn(block, distance):
    size = lax.axis_size("hour")
    return lax.ppermute(block, "hour", [(i, (i + distance) % size) for i in range(size)])


def expander(rows, lags, dtype):
    shape = (rows, rows * lags)
    row = lax.broadcasted_iota(jnp.int32, shape, 0)
    column = lax.broadcasted_iota(jnp.int32, shape, 1)
    first = row * lags
    return ((column >= first) & (column < first + lags)).astype(dtype)


def call(kernel, outs, operands, spaces, scratch=(), limit=SMALL_LIMIT, flops=0, moved=0, name=None):
    where = {"v": pltpu.VMEM, "s": pltpu.SMEM, "a": pl.ANY}
    vmem = pl.BlockSpec(memory_space=pltpu.VMEM)
    return pl.pallas_call(
        kernel,
        in_specs=[pl.BlockSpec(memory_space=where[c]) for c in spaces],
        out_specs=[vmem] * len(outs),
        out_shape=[jax.ShapeDtypeStruct(shape, dtype) for shape, dtype in outs],
        scratch_shapes=scratch,
        compiler_params=pltpu.CompilerParams(vmem_limit_bytes=limit),
        cost_estimate=pl.CostEstimate(flops=flops, bytes_accessed=moved, transcendentals=0),
        name=name,
    )(*operands)


def prepare_kernel(devices, first, foot_hbm, mask_ref, after_ref, masked_ref, foot_ref, sems):
    del after_ref
    me = lax.axis_index("rcpt")
    blocks, lags, tiles = mask_ref.shape
    depth, cells = foot_ref.shape
    own = cells // devices
    tile = cells // tiles
    group = 2 * lags
    part = foot_hbm.shape[0] // blocks
    used = depth // part
    copies = []
    for b in range(used):
        source = foot_hbm.at[pl.ds((first + b) * part, part)]
        copies.append(pltpu.make_async_copy(source, foot_ref.at[pl.ds(b * part, part)], sems.at[b]))
    for copy in copies:
        copy.start()
    mask = mask_ref[first : first + used].astype(F32)
    twice = jnp.broadcast_to(mask[:, None], (used, 2, lags, tiles)).reshape(used * group, tiles)
    wide = jnp.dot(twice.astype(BF16), expander(tiles, tile, BF16), preferred_element_type=F32)
    wide = wide.astype(BF16)
    for b in range(used):
        copies[b].wait()
        for d in range(devices):
            cut = slice(d * own, (d + 1) * own)
            keep = wide[b * group : (b + 1) * group, cut]
            for j in range(part // group):
                at = pl.ds(b * part + j * group, group)
                masked_ref[me ^ d, at, :] = foot_ref[at, cut] * keep


def prepare(foot, mask, after, devices, first, blocks):
    depth, cells = foot.shape
    depth = depth // mask.shape[0] * blocks
    return call(
        functools.partial(prepare_kernel, devices, first),
        [((devices, depth, cells // devices), BF16)],
        [foot, mask, after],
        "ava",
        [pltpu.VMEM((depth, cells), BF16), pltpu.SemaphoreType.DMA((blocks,))],
        limit=VMEM_LIMIT,
        flops=BUSY,
        moved=4 * depth * cells,
        name="prepare",
    )[0]


def choose_kernel(lags, hours, hour_ref, obs_ref, weight_ref, count_ref, after_ref, select_ref, line_ref):
    del after_ref
    rows = hour_ref.shape[1]
    live = (lax.broadcasted_iota(jnp.int32, (1, rows), 1) < count_ref[0]).astype(F32)
    sides = [live * weight_ref[...], obs_ref[...], hour_ref[...].astype(F32)]
    sides = jnp.concatenate([jnp.broadcast_to(side, (8, rows)) for side in sides], axis=0)
    wide = jnp.dot(
        sides,
        expander(rows, lags, F32),
        precision=lax.Precision.HIGHEST,
        preferred_element_type=F32,
    )
    line_ref[...] = wide[: 2 * 8]
    column = lax.broadcasted_iota(jnp.int32, (1, rows * lags), 1)
    hour = wide[2 * 8 : 2 * 8 + 1].astype(jnp.int32) - lax.rem(column, lags)
    slot = jnp.where(hour >= 0, hour, hour + (hours + RIM))
    wanted = lax.broadcasted_iota(jnp.int32, select_ref.shape, 0)
    select_ref[...] = (wanted == slot).astype(F32)


def choose(hour, obs, weight, count, after, lags, hours):
    rows = hour.shape[1]
    return call(
        functools.partial(choose_kernel, lags, hours),
        [((hours + PAIR, rows * lags), F32), ((2 * 8, rows * lags), F32)],
        [hour, obs, weight, count, after],
        "vvvsa",
        flops=BUSY,
        name="choose",
    )


def tails_kernel(low_ref, far_ref, after_ref, out_ref):
    del after_ref
    hours = low_ref.shape[0]
    ends = [ref[hours - PAIR :].astype(F32)[RIM:] for ref in (low_ref, far_ref)]
    out_ref[...] = jnp.concatenate(ends, axis=0).astype(BF16)


def tails(low, far_low, after):
    outs = [((PAIR, low.shape[1]), BF16)]
    return call(tails_kernel, outs, [low, far_low, after], "vva", name="tails")[0]


def window_kernel(low_ref, far_ref, rims_ref, after_ref, out_ref):
    del after_ref
    hours = low_ref.shape[0]
    inside = (lax.axis_index("hour") > 0).astype(F32)
    out_ref[:hours] = low_ref[...]
    out_ref[hours : 2 * hours] = far_ref[...]
    out_ref[2 * hours :] = (rims_ref[...].astype(F32) * inside).astype(BF16)


def window(low, far_low, rims, after):
    hours, columns = low.shape
    outs = [((2 * hours + PAIR, columns), BF16)]
    return call(window_kernel, outs, [low, far_low, rims, after], "vvva", name="window")[0]


def pack_kernel(*refs):
    *parts, _, out_ref = refs
    height = parts[0].shape[0]
    for i, part in enumerate(parts):
        out_ref[i * height : (i + 1) * height] = part[...]


def pack(parts, after):
    height, columns = parts[0].shape
    outs = [((len(parts) * height, columns), BF16)]
    operands = [*parts, after]
    return call(pack_kernel, outs, operands, "v" * len(operands), name="pack")[0]


def row_spans(masked_refs):
    spans, at = [], 0
    for masked_ref in masked_refs:
        spans.append(slice(at, at + masked_ref.shape[1]))
        at += masked_ref.shape[1]
    return spans


def add_scores(windows, masked_refs, start, score_ref, window_ref):
    hours = window_ref.shape[0] - PAIR
    half = masked_refs[0].shape[0] // 2
    spans = row_spans(masked_refs)
    for i, read in enumerate(windows):
        rims = read(slice(2 * hours, 2 * hours + PAIR)).astype(F32)
        gap = jnp.zeros_like(rims[:RIM])
        for j in range(2):
            window_ref[:hours] = read(slice(j * hours, (j + 1) * hours))
            rim = rims[j * RIM : (j + 1) * RIM]
            window_ref[hours:] = jnp.concatenate([rim, gap], axis=0).astype(BF16)
            k = (j * half + 2 * i) ^ start
            dims = (((1,), (1,)), ((), ()))
            for at, masked_ref in zip(spans, masked_refs):
                term = lax.dot_general(
                    window_ref[...], masked_ref[k], dims, preferred_element_type=F32
                )
                if start == 0 and i == 0 and j == 0:
                    score_ref[:, at] = term
                else:
                    score_ref[:, at] += term


def readers(first_ref, rest_ref):
    height = first_ref.shape[0]

    def read(i, rows):
        if i == 0:
            return first_ref[rows]
        return rest_ref[(i - 1) * height + rows.start : (i - 1) * height + rows.stop]

    count = 1 + rest_ref.shape[0] // height
    return [functools.partial(read, i) for i in range(count)]


def score_kernel(first_ref, rest_ref, top_ref, low_ref, score_ref, window_ref):
    add_scores(readers(first_ref, rest_ref), (top_ref, low_ref), 0, score_ref, window_ref)


def score(first, rest, masked):
    devices, _, own = masked[0].shape
    depth = sum(part.shape[1] for part in masked)
    width = first.shape[0] // 2 - RIM + PAIR
    return call(
        score_kernel,
        [((width, depth), F32)],
        [first, rest, *masked],
        "vvvv",
        [pltpu.VMEM((width, own), BF16)],
        flops=width * depth * own * devices,
        moved=depth * own * devices,
        name="score",
    )[0]


def terms(spread_ref, masked_refs, k):
    total = None
    for at, masked_ref in zip(row_spans(masked_refs), masked_refs):
        term = jnp.dot(spread_ref[:, at], masked_ref[k], preferred_element_type=F32)
        total = term if total is None else total + term
    return total


def group_sums(values, lags):
    lane = lax.broadcasted_iota(jnp.int32, values.shape, 1)
    size = values.shape[1]
    step = 1
    while step < lags:
        up, down = pltpu.roll(values, step, 1), pltpu.roll(values, size - step, 1)
        values = values + jnp.where((lane & step) != 0, up, down)
        step *= 2
    return values


def adjoint_kernel(
    lags, first_ref, rest_ref, top_ref, low_ref, begun_ref, select_ref, line_ref,
    mism_ref, spread_ref, other_ref, score_ref, window_ref,
):
    width, depth = score_ref.shape
    score_ref[...] = begun_ref[...]
    add_scores(readers(first_ref, rest_ref), (top_ref, low_ref), 1, score_ref, window_ref)
    line = jnp.sum(score_ref[...] * select_ref[...], axis=0, keepdims=True)
    model = group_sums(jnp.broadcast_to(line, (8, depth)), lags)
    mism = line_ref[:8] * (model - line_ref[8:])
    mism_ref[...] = mism
    weighted = mism.astype(BF16).astype(F32)
    for i in range(0, width, PAIR):
        rows = [select_ref[i + j : i + j + 8] * weighted for j in (0, 8)]
        spread_ref[i : i + PAIR] = jnp.concatenate(rows, axis=0).astype(BF16)
    for k in range(top_ref.shape[0] // 2):
        other_ref[k] = terms(spread_ref, (top_ref, low_ref), 2 * k + 1).astype(BF16)


def adjoint(first, rest, masked, begun, select, lines, lags):
    devices, _, own = masked[0].shape
    depth = sum(part.shape[1] for part in masked)
    width = begun.shape[0]
    return call(
        functools.partial(adjoint_kernel, lags),
        [
            ((8, depth), F32),
            ((width, depth), BF16),
            ((devices // 2, width, own), BF16),
        ],
        [first, rest, *masked, begun, select, lines],
        "v" * 7,
        [pltpu.VMEM((width, depth), F32), pltpu.VMEM((width, own), BF16)],
        flops=2 * width * depth * own * devices,
        moved=depth * own * devices,
        name="adjoint",
    )


def mine_kernel(spread_ref, top_ref, low_ref, own_ref):
    for k in range(top_ref.shape[0] // 2):
        own_ref[k] = terms(spread_ref, (top_ref, low_ref), 2 * k)


def mine_part(spread, masked):
    devices, _, own = masked[0].shape
    depth = sum(part.shape[1] for part in masked)
    width = spread.shape[0]
    return call(
        mine_kernel,
        [((devices // 2, width, own), F32)],
        [spread, *masked],
        "vvv",
        flops=width * depth * own * devices,
        moved=depth * own * devices,
        name="mine",
    )[0]


def narrow_kernel(mism_ref, after_ref, out_ref):
    del after_ref
    rows, depth = out_ref.shape[1], mism_ref.shape[1]
    row, column = (lax.broadcasted_iota(jnp.int32, (rows, depth), i) for i in range(2))
    first = (column == row * (depth // rows)).astype(F32)
    narrow = lax.dot_general(
        mism_ref[...],
        first,
        (((1,), (1,)), ((), ())),
        precision=lax.Precision.HIGHEST,
        preferred_element_type=F32,
    )
    out_ref[...] = narrow[:1]


def narrow(mism, after, rows):
    outs = [((1, rows), F32)]
    return call(narrow_kernel, outs, [mism, after], "va", flops=BUSY, name="narrow")[0]


def join_kernel(own_ref, came_ref, main_ref, rims_ref):
    half, width, _ = own_ref.shape
    hours = width - PAIR
    for i in range(half // 2):
        edges = []
        for j in range(2):
            k = i + j * (half // 2)
            total = own_ref[k] + came_ref[k].astype(F32)
            main_ref[i, j * hours : (j + 1) * hours] = total[:hours]
            edges.append(total[hours : hours + RIM])
        rims_ref[i * PAIR : (i + 1) * PAIR] = jnp.concatenate(edges, axis=0).astype(BF16)


def join(own, came):
    half, width, columns = own.shape
    outs = [
        ((half // 2, 2 * (width - PAIR), columns), F32),
        ((half // 2 * PAIR, columns), BF16),
    ]
    return call(join_kernel, outs, [own, came], "vv", name="join")


def with_rims(main_ref, rims_ref, i, j):
    hours = main_ref.shape[1] // 2
    inside = (lax.axis_index("hour") < lax.axis_size("hour") - 1).astype(F32)
    rims = rims_ref[i * PAIR : (i + 1) * PAIR].astype(F32) * inside
    at = (j + 1) * hours - RIM
    last = main_ref[i, at : at + RIM] + rims[j * RIM : (j + 1) * RIM]
    return jnp.concatenate([main_ref[i, j * hours : at], last], axis=0)


def shares_kernel(j, main_ref, rims_ref, after_ref, first_ref, *outs):
    del after_ref
    first_ref[...] = with_rims(main_ref, rims_ref, 0, j)
    for i, out in enumerate(outs):
        out[...] = with_rims(main_ref, rims_ref, i + 1, j).astype(BF16)


def shares(main, rims, j, after):
    count, both, columns = main.shape
    shape = (both // 2, columns)
    outs = [(shape, F32)] + [(shape, BF16)] * (count - 1)
    first, *parts = call(
        functools.partial(shares_kernel, j), outs, [main, rims, after], "vva", flops=BUSY, name="shares"
    )
    return first, parts


def outward_kernel(first_ref, *refs):
    *arrived, out_ref = refs
    total = first_ref[...]
    for piece in arrived:
        total += piece[...].astype(F32)
    out_ref[...] = total.astype(out_ref.dtype)


def outward(first, arrived, dtype):
    operands = [first, *arrived]
    outs = [(first.shape, dtype)]
    return call(outward_kernel, outs, operands, "v" * len(operands), name="outward")[0]


def per_device(flux, footprint, tile_mask, rec_hour, observed, obs_weight, site_count):
    hours, own = flux.shape
    rows, lags, cells = footprint.shape
    devices = cells // own
    far = devices // 2
    near = range(2, far, 2)

    low = flux.astype(BF16)
    far_low = swap(low, far)
    foot = footprint.reshape(rows * lags, cells)
    blocks = tile_mask.shape[0]
    head = blocks * 5 // 8
    top = prepare(foot, tile_mask, low, devices, 0, head)
    ends = tails(low, far_low, top)
    bottom = prepare(foot, tile_mask, ends, devices, head, blocks - head)
    first = window(low, far_low, turn(ends, 1), bottom)
    parts = [swap(first, k) for k in range(2, far, 2)]
    other_first = swap(first, 1)
    select, lines = choose(
        rec_hour.reshape(1, rows),
        observed.reshape(1, rows),
        obs_weight.reshape(1, rows),
        site_count,
        first,
        lags,
        hours,
    )
    rest = pack(parts, lines)
    masked = (top, bottom)
    begun = score(first, rest, masked)
    mism, spread, other = adjoint(
        other_first, swap(rest, 1), masked, begun, select, lines, lags
    )

    main, rims = join(mine_part(spread, masked), swap(other, 1))
    back = turn(rims, -1)
    far_sum, parts = shares(main, back, 1, rims)
    passed = [swap(part, k) for part, k in zip(parts, near)]
    near_sum, others = shares(main, back, 0, parts[0])
    arrived = [swap(part, k) for part, k in zip(others, near)]
    mism = narrow(mism, far_sum, rows)
    relay = outward(far_sum, passed, BF16)
    total = outward(near_sum, arrived, F32)
    gradient = total + swap(relay, far).astype(F32)
    return (gradient, mism.reshape(rows))


def solution(mesh):
    placed = (
        P("hour", "rcpt"),
        P(("hour", "rcpt"), None, None),
        P(("hour", "rcpt"), None, None),
        P(("hour", "rcpt")),
        P(("hour", "rcpt")),
        P(("hour", "rcpt")),
        P(("hour", "rcpt")),
    )
    return jax.shard_map(
        per_device,
        mesh=mesh,
        in_specs=placed,
        out_specs=(P("hour", "rcpt"), P(("hour", "rcpt"))),
        check_vma=False,
    )
```

```python
import functools

import jax
import jax.numpy as jnp
from jax import lax
from jax.experimental import pallas as pl
from jax.experimental.pallas import tpu as pltpu
from jax.sharding import PartitionSpec as P

RIM = 8
PAIR = 2 * RIM
F32 = jnp.float32
BF16 = jnp.bfloat16
VMEM_LIMIT = 44 * 1024 * 1024
SMALL_LIMIT = 8 * 1024 * 1024
BUSY = 10**10


def swap(block, bit):
    devices = range(lax.axis_size("rcpt"))
    return lax.ppermute(block, "rcpt", [(i, i ^ bit) for i in devices])


def turn(block, distance):
    size = lax.axis_size("hour")
    return lax.ppermute(block, "hour", [(i, (i + distance) % size) for i in range(size)])


def expander(rows, lags, dtype):
    shape = (rows, rows * lags)
    row = lax.broadcasted_iota(jnp.int32, shape, 0)
    column = lax.broadcasted_iota(jnp.int32, shape, 1)
    first = row * lags
    return ((column >= first) & (column < first + lags)).astype(dtype)


def call(kernel, outs, operands, spaces, scratch=(), limit=SMALL_LIMIT, flops=0, moved=0, name=None):
    where = {"v": pltpu.VMEM, "s": pltpu.SMEM, "a": pl.ANY}
    vmem = pl.BlockSpec(memory_space=pltpu.VMEM)
    return pl.pallas_call(
        kernel,
        in_specs=[pl.BlockSpec(memory_space=where[c]) for c in spaces],
        out_specs=[vmem] * len(outs),
        out_shape=[jax.ShapeDtypeStruct(shape, dtype) for shape, dtype in outs],
        scratch_shapes=scratch,
        compiler_params=pltpu.CompilerParams(vmem_limit_bytes=limit),
        cost_estimate=pl.CostEstimate(flops=flops, bytes_accessed=moved, transcendentals=0),
        name=name,
    )(*operands)


def prepare_kernel(devices, first, foot_hbm, mask_ref, after_ref, masked_ref, foot_ref, sems):
    del after_ref
    me = lax.axis_index("rcpt")
    blocks, lags, tiles = mask_ref.shape
    depth, cells = foot_ref.shape
    own = cells // devices
    tile = cells // tiles
    group = 2 * lags
    part = foot_hbm.shape[0] // blocks
    used = depth // part
    copies = []
    for b in range(used):
        source = foot_hbm.at[pl.ds((first + b) * part, part)]
        copies.append(pltpu.make_async_copy(source, foot_ref.at[pl.ds(b * part, part)], sems.at[b]))
    for copy in copies:
        copy.start()
    mask = mask_ref[first : first + used].astype(F32)
    twice = jnp.broadcast_to(mask[:, None], (used, 2, lags, tiles)).reshape(used * group, tiles)
    wide = jnp.dot(twice.astype(BF16), expander(tiles, tile, BF16), preferred_element_type=F32)
    wide = wide.astype(BF16)
    for b in range(used):
        copies[b].wait()
        for d in range(devices):
            cut = slice(d * own, (d + 1) * own)
            keep = wide[b * group : (b + 1) * group, cut]
            for j in range(part // group):
                at = pl.ds(b * part + j * group, group)
                masked_ref[me ^ d, at, :] = foot_ref[at, cut] * keep


def prepare(foot, mask, after, devices, first, blocks):
    depth, cells = foot.shape
    depth = depth // mask.shape[0] * blocks
    return call(
        functools.partial(prepare_kernel, devices, first),
        [((devices, depth, cells // devices), BF16)],
        [foot, mask, after],
        "ava",
        [pltpu.VMEM((depth, cells), BF16), pltpu.SemaphoreType.DMA((blocks,))],
        limit=VMEM_LIMIT,
        flops=BUSY,
        moved=4 * depth * cells,
        name="prepare",
    )[0]


def choose_kernel(lags, hours, hour_ref, obs_ref, weight_ref, count_ref, after_ref, select_ref, line_ref):
    del after_ref
    rows = hour_ref.shape[1]
    live = (lax.broadcasted_iota(jnp.int32, (1, rows), 1) < count_ref[0]).astype(F32)
    sides = [live * weight_ref[...], obs_ref[...], hour_ref[...].astype(F32)]
    sides = jnp.concatenate([jnp.broadcast_to(side, (8, rows)) for side in sides], axis=0)
    wide = jnp.dot(
        sides,
        expander(rows, lags, F32),
        precision=lax.Precision.HIGHEST,
        preferred_element_type=F32,
    )
    line_ref[...] = wide[: 2 * 8]
    column = lax.broadcasted_iota(jnp.int32, (1, rows * lags), 1)
    hour = wide[2 * 8 : 2 * 8 + 1].astype(jnp.int32) - lax.rem(column, lags)
    slot = jnp.where(hour >= 0, hour, hour + (hours + RIM))
    wanted = lax.broadcasted_iota(jnp.int32, select_ref.shape, 0)
    select_ref[...] = (wanted == slot).astype(F32)


def choose(hour, obs, weight, count, after, lags, hours):
    rows = hour.shape[1]
    return call(
        functools.partial(choose_kernel, lags, hours),
        [((hours + PAIR, rows * lags), F32), ((2 * 8, rows * lags), F32)],
        [hour, obs, weight, count, after],
        "vvvsa",
        flops=BUSY,
        name="choose",
    )


def tails_kernel(low_ref, far_ref, after_ref, out_ref):
    del after_ref
    hours = low_ref.shape[0]
    ends = [ref[hours - PAIR :].astype(F32)[RIM:] for ref in (low_ref, far_ref)]
    out_ref[...] = jnp.concatenate(ends, axis=0).astype(BF16)


def tails(low, far_low, after):
    outs = [((PAIR, low.shape[1]), BF16)]
    return call(tails_kernel, outs, [low, far_low, after], "vva", name="tails")[0]


def window_kernel(low_ref, far_ref, rims_ref, after_ref, out_ref):
    del after_ref
    hours = low_ref.shape[0]
    inside = (lax.axis_index("hour") > 0).astype(F32)
    out_ref[:hours] = low_ref[...]
    out_ref[hours : 2 * hours] = far_ref[...]
    out_ref[2 * hours :] = (rims_ref[...].astype(F32) * inside).astype(BF16)


def window(low, far_low, rims, after):
    hours, columns = low.shape
    outs = [((2 * hours + PAIR, columns), BF16)]
    return call(window_kernel, outs, [low, far_low, rims, after], "vvva", name="window")[0]


def pack_kernel(*refs):
    *parts, _, out_ref = refs
    height = parts[0].shape[0]
    for i, part in enumerate(parts):
        out_ref[i * height : (i + 1) * height] = part[...]


def pack(parts, after):
    height, columns = parts[0].shape
    outs = [((len(parts) * height, columns), BF16)]
    operands = [*parts, after]
    return call(pack_kernel, outs, operands, "v" * len(operands), name="pack")[0]


def row_spans(masked_refs):
    spans, at = [], 0
    for masked_ref in masked_refs:
        spans.append(slice(at, at + masked_ref.shape[1]))
        at += masked_ref.shape[1]
    return spans


def add_scores(windows, masked_refs, start, score_ref, window_ref):
    hours = window_ref.shape[0] - PAIR
    half = masked_refs[0].shape[0] // 2
    spans = row_spans(masked_refs)
    for i, read in enumerate(windows):
        rims = read(slice(2 * hours, 2 * hours + PAIR)).astype(F32)
        gap = jnp.zeros_like(rims[:RIM])
        for j in range(2):
            window_ref[:hours] = read(slice(j * hours, (j + 1) * hours))
            rim = rims[j * RIM : (j + 1) * RIM]
            window_ref[hours:] = jnp.concatenate([rim, gap], axis=0).astype(BF16)
            k = (j * half + 2 * i) ^ start
            dims = (((1,), (1,)), ((), ()))
            for at, masked_ref in zip(spans, masked_refs):
                term = lax.dot_general(
                    window_ref[...], masked_ref[k], dims, preferred_element_type=F32
                )
                if start == 0 and i == 0 and j == 0:
                    score_ref[:, at] = term
                else:
                    score_ref[:, at] += term


def readers(first_ref, rest_ref):
    height = first_ref.shape[0]

    def read(i, rows):
        if i == 0:
            return first_ref[rows]
        return rest_ref[(i - 1) * height + rows.start : (i - 1) * height + rows.stop]

    count = 1 + rest_ref.shape[0] // height
    return [functools.partial(read, i) for i in range(count)]


def score_kernel(first_ref, rest_ref, top_ref, low_ref, score_ref, window_ref):
    add_scores(readers(first_ref, rest_ref), (top_ref, low_ref), 0, score_ref, window_ref)


def score(first, rest, masked):
    devices, _, own = masked[0].shape
    depth = sum(part.shape[1] for part in masked)
    width = first.shape[0] // 2 - RIM + PAIR
    return call(
        score_kernel,
        [((width, depth), F32)],
        [first, rest, *masked],
        "vvvv",
        [pltpu.VMEM((width, own), BF16)],
        flops=width * depth * own * devices,
        moved=depth * own * devices,
        name="score",
    )[0]


def terms(spread_ref, masked_refs, k):
    total = None
    for at, masked_ref in zip(row_spans(masked_refs), masked_refs):
        term = jnp.dot(spread_ref[:, at], masked_ref[k], preferred_element_type=F32)
        total = term if total is None else total + term
    return total


def group_sums(values, lags):
    lane = lax.broadcasted_iota(jnp.int32, values.shape, 1)
    size = values.shape[1]
    step = 1
    while step < lags:
        up, down = pltpu.roll(values, step, 1), pltpu.roll(values, size - step, 1)
        values = values + jnp.where((lane & step) != 0, up, down)
        step *= 2
    return values


def adjoint_kernel(
    lags, first_ref, rest_ref, top_ref, low_ref, begun_ref, select_ref, line_ref,
    mism_ref, spread_ref, other_ref, rims_ref, score_ref, window_ref,
):
    width, depth = score_ref.shape
    hours = other_ref.shape[1]
    score_ref[...] = begun_ref[...]
    add_scores(readers(first_ref, rest_ref), (top_ref, low_ref), 1, score_ref, window_ref)
    line = jnp.sum(score_ref[...] * select_ref[...], axis=0, keepdims=True)
    model = group_sums(jnp.broadcast_to(line, (8, depth)), lags)
    mism = line_ref[:8] * (model - line_ref[8:])
    mism_ref[...] = mism
    weighted = mism.astype(BF16).astype(F32)
    for i in range(0, width, PAIR):
        rows = [select_ref[i + j : i + j + 8] * weighted for j in (0, 8)]
        spread_ref[i : i + PAIR] = jnp.concatenate(rows, axis=0).astype(BF16)
    count = top_ref.shape[0] // 4
    for i in range(count):
        edges = []
        for k in (i, i + count):
            term = terms(spread_ref, (top_ref, low_ref), 2 * k + 1)
            other_ref[k] = term[:hours].astype(BF16)
            edges.append(term[hours : hours + RIM])
        rims_ref[i * PAIR : (i + 1) * PAIR] = jnp.concatenate(edges, axis=0).astype(BF16)


def adjoint(first, rest, masked, begun, select, lines, lags):
    devices, _, own = masked[0].shape
    depth = sum(part.shape[1] for part in masked)
    width = begun.shape[0]
    return call(
        functools.partial(adjoint_kernel, lags),
        [
            ((8, depth), F32),
            ((width, depth), BF16),
            ((devices // 2, width - PAIR, own), BF16),
            ((devices // 4 * PAIR, own), BF16),
        ],
        [first, rest, *masked, begun, select, lines],
        "v" * 7,
        [pltpu.VMEM((width, depth), F32), pltpu.VMEM((width, own), BF16)],
        flops=2 * width * depth * own * devices,
        moved=depth * own * devices,
        name="adjoint",
    )


def mine_kernel(spread_ref, top_ref, low_ref, own_ref, rims_ref):
    count = top_ref.shape[0] // 4
    hours = own_ref.shape[1]
    for i in range(count):
        edges = []
        for k in (i, i + count):
            term = terms(spread_ref, (top_ref, low_ref), 2 * k)
            own_ref[k] = term[:hours]
            edges.append(term[hours : hours + RIM])
        rims_ref[i * PAIR : (i + 1) * PAIR] = jnp.concatenate(edges, axis=0)


def mine_part(spread, masked):
    devices, _, own = masked[0].shape
    depth = sum(part.shape[1] for part in masked)
    width = spread.shape[0]
    return call(
        mine_kernel,
        [((devices // 2, width - PAIR, own), F32), ((devices // 4 * PAIR, own), F32)],
        [spread, *masked],
        "vvv",
        flops=width * depth * own * devices,
        moved=depth * own * devices,
        name="mine",
    )


def narrow_kernel(mism_ref, after_ref, out_ref):
    del after_ref
    rows, depth = out_ref.shape[1], mism_ref.shape[1]
    row, column = (lax.broadcasted_iota(jnp.int32, (rows, depth), i) for i in range(2))
    first = (column == row * (depth // rows)).astype(F32)
    narrow = lax.dot_general(
        mism_ref[...],
        first,
        (((1,), (1,)), ((), ())),
        precision=lax.Precision.HIGHEST,
        preferred_element_type=F32,
    )
    out_ref[...] = narrow[:1]


def narrow(mism, after, rows):
    outs = [((1, rows), F32)]
    return call(narrow_kernel, outs, [mism, after], "va", flops=BUSY, name="narrow")[0]


def gate_kernel(rows_ref, after_ref, out_ref):
    del after_ref
    out_ref[...] = rows_ref[...]


def gate(rows, after):
    outs = [(rows.shape, rows.dtype)]
    return call(gate_kernel, outs, [rows, after], "va", name="gate")[0]


def join_rims_kernel(own_ref, came_ref, out_ref):
    out_ref[...] = (own_ref[...] + came_ref[...].astype(F32)).astype(BF16)


def join_rims(own, came):
    return call(join_rims_kernel, [(own.shape, BF16)], [own, came], "vv", name="rims")[0]


def join_kernel(own_ref, came_ref, after_ref, main_ref):
    del after_ref
    half, hours, _ = own_ref.shape
    for i in range(half // 2):
        for j in range(2):
            k = i + j * (half // 2)
            main_ref[i, j * hours : (j + 1) * hours] = own_ref[k] + came_ref[k].astype(F32)


def join(own, came, after):
    half, hours, columns = own.shape
    outs = [((half // 2, 2 * hours, columns), F32)]
    return call(join_kernel, outs, [own, came, after], "vva", flops=BUSY, name="join")[0]


def with_rims(main_ref, rims_ref, i, j):
    hours = main_ref.shape[1] // 2
    inside = (lax.axis_index("hour") < lax.axis_size("hour") - 1).astype(F32)
    rims = rims_ref[i * PAIR : (i + 1) * PAIR].astype(F32) * inside
    at = (j + 1) * hours - RIM
    last = main_ref[i, at : at + RIM] + rims[j * RIM : (j + 1) * RIM]
    return jnp.concatenate([main_ref[i, j * hours : at], last], axis=0)


def shares_kernel(j, main_ref, rims_ref, after_ref, first_ref, *outs):
    del after_ref
    first_ref[...] = with_rims(main_ref, rims_ref, 0, j)
    for i, out in enumerate(outs):
        out[...] = with_rims(main_ref, rims_ref, i + 1, j).astype(BF16)


def shares(main, rims, j, after):
    count, both, columns = main.shape
    shape = (both // 2, columns)
    outs = [(shape, F32)] + [(shape, BF16)] * (count - 1)
    first, *parts = call(
        functools.partial(shares_kernel, j), outs, [main, rims, after], "vva", flops=BUSY, name="shares"
    )
    return first, parts


def outward_kernel(first_ref, *refs):
    *arrived, out_ref = refs
    total = first_ref[...]
    for piece in arrived:
        total += piece[...].astype(F32)
    out_ref[...] = total.astype(out_ref.dtype)


def outward(first, arrived, dtype):
    operands = [first, *arrived]
    outs = [(first.shape, dtype)]
    return call(outward_kernel, outs, operands, "v" * len(operands), name="outward")[0]


def per_device(flux, footprint, tile_mask, rec_hour, observed, obs_weight, site_count):
    hours, own = flux.shape
    rows, lags, cells = footprint.shape
    devices = cells // own
    far = devices // 2
    near = range(2, far, 2)

    low = flux.astype(BF16)
    far_low = swap(low, far)
    foot = footprint.reshape(rows * lags, cells)
    blocks = tile_mask.shape[0]
    head = blocks * 5 // 8
    top = prepare(foot, tile_mask, low, devices, 0, head)
    ends = tails(low, far_low, top)
    bottom = prepare(foot, tile_mask, ends, devices, head, blocks - head)
    first = window(low, far_low, turn(ends, 1), bottom)
    parts = [swap(first, k) for k in range(2, far, 2)]
    other_first = swap(first, 1)
    select, lines = choose(
        rec_hour.reshape(1, rows),
        observed.reshape(1, rows),
        obs_weight.reshape(1, rows),
        site_count,
        first,
        lags,
        hours,
    )
    rest = pack(parts, lines)
    masked = (top, bottom)
    begun = score(first, rest, masked)
    mism, spread, other, other_rims = adjoint(
        other_first, swap(rest, 1), masked, begun, select, lines, lags
    )

    came_rims = swap(other_rims, 1)
    own_part, own_rims = mine_part(spread, masked)
    rims = join_rims(own_rims, came_rims)
    came = swap(gate(other, rims), 1)
    back = turn(rims, -1)
    main = join(own_part, came, rims)
    far_sum, parts = shares(main, back, 1, rims)
    passed = [swap(part, k) for part, k in zip(parts, near)]
    near_sum, others = shares(main, back, 0, parts[0])
    arrived = [swap(part, k) for part, k in zip(others, near)]
    mism = narrow(mism, far_sum, rows)
    relay = outward(far_sum, passed, BF16)
    total = outward(near_sum, arrived, F32)
    gradient = total + swap(relay, far).astype(F32)
    return (gradient, mism.reshape(rows))


def solution(mesh):
    placed = (
        P("hour", "rcpt"),
        P(("hour", "rcpt"), None, None),
        P(("hour", "rcpt"), None, None),
        P(("hour", "rcpt")),
        P(("hour", "rcpt")),
        P(("hour", "rcpt")),
        P(("hour", "rcpt")),
    )
    return jax.shard_map(
        per_device,
        mesh=mesh,
        in_specs=placed,
        out_specs=(P("hour", "rcpt"), P(("hour", "rcpt"))),
        check_vma=False,
    )
```

```python
import functools

import jax
import jax.numpy as jnp
from jax import lax
from jax.experimental import pallas as pl
from jax.experimental.pallas import tpu as pltpu
from jax.sharding import PartitionSpec as P

RIM = 8
PAIR = 2 * RIM
F32 = jnp.float32
BF16 = jnp.bfloat16
VMEM_LIMIT = 44 * 1024 * 1024
SMALL_LIMIT = 8 * 1024 * 1024
BUSY = 10**10


def swap(block, bit):
    devices = range(lax.axis_size("rcpt"))
    return lax.ppermute(block, "rcpt", [(i, i ^ bit) for i in devices])


def turn(block, distance):
    size = lax.axis_size("hour")
    return lax.ppermute(block, "hour", [(i, (i + distance) % size) for i in range(size)])


def expander(rows, lags, dtype):
    shape = (rows, rows * lags)
    row = lax.broadcasted_iota(jnp.int32, shape, 0)
    column = lax.broadcasted_iota(jnp.int32, shape, 1)
    first = row * lags
    return ((column >= first) & (column < first + lags)).astype(dtype)


def call(kernel, outs, operands, spaces, scratch=(), limit=SMALL_LIMIT, flops=0, moved=0, name=None):
    where = {"v": pltpu.VMEM, "s": pltpu.SMEM, "a": pl.ANY}
    vmem = pl.BlockSpec(memory_space=pltpu.VMEM)
    return pl.pallas_call(
        kernel,
        in_specs=[pl.BlockSpec(memory_space=where[c]) for c in spaces],
        out_specs=[vmem] * len(outs),
        out_shape=[jax.ShapeDtypeStruct(shape, dtype) for shape, dtype in outs],
        scratch_shapes=scratch,
        compiler_params=pltpu.CompilerParams(vmem_limit_bytes=limit),
        cost_estimate=pl.CostEstimate(flops=flops, bytes_accessed=moved, transcendentals=0),
        name=name,
    )(*operands)


def prepare_kernel(devices, first, foot_hbm, mask_ref, after_ref, masked_ref, foot_ref, sems):
    del after_ref
    me = lax.axis_index("rcpt")
    blocks, lags, tiles = mask_ref.shape
    depth, cells = foot_ref.shape
    own = cells // devices
    tile = cells // tiles
    group = 2 * lags
    part = foot_hbm.shape[0] // blocks
    used = depth // part
    copies = []
    for b in range(used):
        source = foot_hbm.at[pl.ds((first + b) * part, part)]
        copies.append(pltpu.make_async_copy(source, foot_ref.at[pl.ds(b * part, part)], sems.at[b]))
    for copy in copies:
        copy.start()
    mask = mask_ref[first : first + used].astype(F32)
    twice = jnp.broadcast_to(mask[:, None], (used, 2, lags, tiles)).reshape(used * group, tiles)
    wide = jnp.dot(twice.astype(BF16), expander(tiles, tile, BF16), preferred_element_type=F32)
    wide = wide.astype(BF16)
    for b in range(used):
        copies[b].wait()
        for d in range(devices):
            cut = slice(d * own, (d + 1) * own)
            keep = wide[b * group : (b + 1) * group, cut]
            for j in range(part // group):
                at = pl.ds(b * part + j * group, group)
                masked_ref[me ^ d, at, :] = foot_ref[at, cut] * keep


def prepare(foot, mask, after, devices, first, blocks):
    depth, cells = foot.shape
    depth = depth // mask.shape[0] * blocks
    return call(
        functools.partial(prepare_kernel, devices, first),
        [((devices, depth, cells // devices), BF16)],
        [foot, mask, after],
        "ava",
        [pltpu.VMEM((depth, cells), BF16), pltpu.SemaphoreType.DMA((blocks,))],
        limit=VMEM_LIMIT,
        flops=BUSY,
        moved=4 * depth * cells,
        name="prepare",
    )[0]


def choose_kernel(lags, hours, hour_ref, obs_ref, weight_ref, count_ref, after_ref, select_ref, line_ref):
    del after_ref
    rows = hour_ref.shape[1]
    live = (lax.broadcasted_iota(jnp.int32, (1, rows), 1) < count_ref[0]).astype(F32)
    sides = [live * weight_ref[...], obs_ref[...], hour_ref[...].astype(F32)]
    sides = jnp.concatenate([jnp.broadcast_to(side, (8, rows)) for side in sides], axis=0)
    wide = jnp.dot(
        sides,
        expander(rows, lags, F32),
        precision=lax.Precision.HIGHEST,
        preferred_element_type=F32,
    )
    line_ref[...] = wide[: 2 * 8]
    column = lax.broadcasted_iota(jnp.int32, (1, rows * lags), 1)
    hour = wide[2 * 8 : 2 * 8 + 1].astype(jnp.int32) - lax.rem(column, lags)
    slot = jnp.where(hour >= 0, hour, hour + (hours + RIM))
    wanted = lax.broadcasted_iota(jnp.int32, select_ref.shape, 0)
    select_ref[...] = (wanted == slot).astype(F32)


def choose(hour, obs, weight, count, after, lags, hours):
    rows = hour.shape[1]
    return call(
        functools.partial(choose_kernel, lags, hours),
        [((hours + PAIR, rows * lags), F32), ((2 * 8, rows * lags), F32)],
        [hour, obs, weight, count, after],
        "vvvsa",
        flops=BUSY,
        name="choose",
    )


def tails_kernel(low_ref, far_ref, after_ref, out_ref):
    del after_ref
    hours = low_ref.shape[0]
    ends = [ref[hours - PAIR :].astype(F32)[RIM:] for ref in (low_ref, far_ref)]
    out_ref[...] = jnp.concatenate(ends, axis=0).astype(BF16)


def tails(low, far_low, after):
    outs = [((PAIR, low.shape[1]), BF16)]
    return call(tails_kernel, outs, [low, far_low, after], "vva", name="tails")[0]


def window_kernel(low_ref, far_ref, rims_ref, after_ref, out_ref):
    del after_ref
    hours = low_ref.shape[0]
    inside = (lax.axis_index("hour") > 0).astype(F32)
    out_ref[:hours] = low_ref[...]
    out_ref[hours : 2 * hours] = far_ref[...]
    out_ref[2 * hours :] = (rims_ref[...].astype(F32) * inside).astype(BF16)


def window(low, far_low, rims, after):
    hours, columns = low.shape
    outs = [((2 * hours + PAIR, columns), BF16)]
    return call(window_kernel, outs, [low, far_low, rims, after], "vvva", name="window")[0]


def pack_kernel(count, *refs):
    parts, out_ref = refs[:count], refs[-1]
    height = parts[0].shape[0]
    for i, part in enumerate(parts):
        out_ref[i * height : (i + 1) * height] = part[...]


def pack(parts, *after):
    height, columns = parts[0].shape
    outs = [((len(parts) * height, columns), BF16)]
    spaces = "v" * len(parts) + "a" * len(after)
    kernel = functools.partial(pack_kernel, len(parts))
    return call(kernel, outs, [*parts, *after], spaces, name="pack")[0]


def row_spans(masked_refs):
    spans, at = [], 0
    for masked_ref in masked_refs:
        spans.append(slice(at, at + masked_ref.shape[1]))
        at += masked_ref.shape[1]
    return spans


def add_scores(windows, masked_refs, start, score_ref, window_ref):
    hours = window_ref.shape[0] - PAIR
    half = masked_refs[0].shape[0] // 2
    spans = row_spans(masked_refs)
    for i, read in enumerate(windows):
        rims = read(slice(2 * hours, 2 * hours + PAIR)).astype(F32)
        gap = jnp.zeros_like(rims[:RIM])
        for j in range(2):
            window_ref[:hours] = read(slice(j * hours, (j + 1) * hours))
            rim = rims[j * RIM : (j + 1) * RIM]
            window_ref[hours:] = jnp.concatenate([rim, gap], axis=0).astype(BF16)
            k = (j * half + 2 * i) ^ start
            dims = (((1,), (1,)), ((), ()))
            for at, masked_ref in zip(spans, masked_refs):
                term = lax.dot_general(
                    window_ref[...], masked_ref[k], dims, preferred_element_type=F32
                )
                if start == 0 and i == 0 and j == 0:
                    score_ref[:, at] = term
                else:
                    score_ref[:, at] += term


def readers(first_ref, rest_ref):
    height = first_ref.shape[0]

    def read(i, rows):
        if i == 0:
            return first_ref[rows]
        return rest_ref[(i - 1) * height + rows.start : (i - 1) * height + rows.stop]

    count = 1 + rest_ref.shape[0] // height
    return [functools.partial(read, i) for i in range(count)]


def score_kernel(first_ref, rest_ref, top_ref, low_ref, score_ref, window_ref):
    add_scores(readers(first_ref, rest_ref), (top_ref, low_ref), 0, score_ref, window_ref)


def score(first, rest, masked):
    devices, _, own = masked[0].shape
    depth = sum(part.shape[1] for part in masked)
    width = first.shape[0] // 2 - RIM + PAIR
    return call(
        score_kernel,
        [((width, depth), F32)],
        [first, rest, *masked],
        "vvvv",
        [pltpu.VMEM((width, own), BF16)],
        flops=width * depth * own * devices,
        moved=depth * own * devices,
        name="score",
    )[0]


def terms(spread_ref, masked_refs, k):
    total = None
    for at, masked_ref in zip(row_spans(masked_refs), masked_refs):
        term = jnp.dot(spread_ref[:, at], masked_ref[k], preferred_element_type=F32)
        total = term if total is None else total + term
    return total


def group_sums(values, lags):
    lane = lax.broadcasted_iota(jnp.int32, values.shape, 1)
    size = values.shape[1]
    step = 1
    while step < lags:
        up, down = pltpu.roll(values, step, 1), pltpu.roll(values, size - step, 1)
        values = values + jnp.where((lane & step) != 0, up, down)
        step *= 2
    return values


def adjoint_kernel(
    lags, first_ref, rest_ref, top_ref, low_ref, begun_ref, select_ref, line_ref,
    mism_ref, spread_ref, other_ref, rims_ref, score_ref, window_ref,
):
    width, depth = score_ref.shape
    hours = other_ref.shape[1]
    score_ref[...] = begun_ref[...]
    add_scores(readers(first_ref, rest_ref), (top_ref, low_ref), 1, score_ref, window_ref)
    line = jnp.sum(score_ref[...] * select_ref[...], axis=0, keepdims=True)
    model = group_sums(jnp.broadcast_to(line, (8, depth)), lags)
    mism = line_ref[:8] * (model - line_ref[8:])
    mism_ref[...] = mism
    weighted = mism.astype(BF16).astype(F32)
    for i in range(0, width, PAIR):
        rows = [select_ref[i + j : i + j + 8] * weighted for j in (0, 8)]
        spread_ref[i : i + PAIR] = jnp.concatenate(rows, axis=0).astype(BF16)
    count = top_ref.shape[0] // 4
    for i in range(count):
        edges = []
        for k in (i, i + count):
            term = terms(spread_ref, (top_ref, low_ref), 2 * k + 1)
            other_ref[k] = term[:hours].astype(BF16)
            edges.append(term[hours : hours + RIM])
        rims_ref[i * PAIR : (i + 1) * PAIR] = jnp.concatenate(edges, axis=0).astype(BF16)


def adjoint(first, rest, masked, begun, select, lines, lags):
    devices, _, own = masked[0].shape
    depth = sum(part.shape[1] for part in masked)
    width = begun.shape[0]
    return call(
        functools.partial(adjoint_kernel, lags),
        [
            ((8, depth), F32),
            ((width, depth), BF16),
            ((devices // 2, width - PAIR, own), BF16),
            ((devices // 4 * PAIR, own), BF16),
        ],
        [first, rest, *masked, begun, select, lines],
        "v" * 7,
        [pltpu.VMEM((width, depth), F32), pltpu.VMEM((width, own), BF16)],
        flops=2 * width * depth * own * devices,
        moved=depth * own * devices,
        name="adjoint",
    )


def mine_kernel(spread_ref, top_ref, low_ref, own_ref, rims_ref):
    count = top_ref.shape[0] // 4
    hours = own_ref.shape[1]
    for i in range(count):
        edges = []
        for k in (i, i + count):
            term = terms(spread_ref, (top_ref, low_ref), 2 * k)
            own_ref[k] = term[:hours]
            edges.append(term[hours : hours + RIM])
        rims_ref[i * PAIR : (i + 1) * PAIR] = jnp.concatenate(edges, axis=0)


def mine_part(spread, masked):
    devices, _, own = masked[0].shape
    depth = sum(part.shape[1] for part in masked)
    width = spread.shape[0]
    return call(
        mine_kernel,
        [((devices // 2, width - PAIR, own), F32), ((devices // 4 * PAIR, own), F32)],
        [spread, *masked],
        "vvv",
        flops=width * depth * own * devices,
        moved=depth * own * devices,
        name="mine",
    )


def narrow_kernel(mism_ref, after_ref, out_ref):
    del after_ref
    rows, depth = out_ref.shape[1], mism_ref.shape[1]
    row, column = (lax.broadcasted_iota(jnp.int32, (rows, depth), i) for i in range(2))
    first = (column == row * (depth // rows)).astype(F32)
    narrow = lax.dot_general(
        mism_ref[...],
        first,
        (((1,), (1,)), ((), ())),
        precision=lax.Precision.HIGHEST,
        preferred_element_type=F32,
    )
    out_ref[...] = narrow[:1]


def narrow(mism, after, rows):
    outs = [((1, rows), F32)]
    return call(narrow_kernel, outs, [mism, after], "va", flops=BUSY, name="narrow")[0]


def gate_kernel(rows_ref, after_ref, out_ref):
    del after_ref
    out_ref[...] = rows_ref[...]


def gate(rows, after):
    outs = [(rows.shape, rows.dtype)]
    return call(gate_kernel, outs, [rows, after], "va", name="gate")[0]


def join_rims_kernel(own_ref, came_ref, out_ref):
    out_ref[...] = (own_ref[...] + came_ref[...].astype(F32)).astype(BF16)


def join_rims(own, came):
    return call(join_rims_kernel, [(own.shape, BF16)], [own, came], "vv", name="rims")[0]


def join_kernel(own_ref, came_ref, after_ref, main_ref):
    del after_ref
    half, hours, _ = own_ref.shape
    for i in range(half // 2):
        for j in range(2):
            k = i + j * (half // 2)
            main_ref[i, j * hours : (j + 1) * hours] = own_ref[k] + came_ref[k].astype(F32)


def join(own, came, after):
    half, hours, columns = own.shape
    outs = [((half // 2, 2 * hours, columns), F32)]
    return call(join_kernel, outs, [own, came, after], "vva", flops=BUSY, name="join")[0]


def with_rims(main_ref, rims_ref, i, j):
    hours = main_ref.shape[1] // 2
    inside = (lax.axis_index("hour") < lax.axis_size("hour") - 1).astype(F32)
    rims = rims_ref[i * PAIR : (i + 1) * PAIR].astype(F32) * inside
    at = (j + 1) * hours - RIM
    last = main_ref[i, at : at + RIM] + rims[j * RIM : (j + 1) * RIM]
    return jnp.concatenate([main_ref[i, j * hours : at], last], axis=0)


def shares_kernel(j, main_ref, rims_ref, after_ref, first_ref, *outs):
    del after_ref
    first_ref[...] = with_rims(main_ref, rims_ref, 0, j)
    for i, out in enumerate(outs):
        out[...] = with_rims(main_ref, rims_ref, i + 1, j).astype(BF16)


def shares(main, rims, j, after):
    count, both, columns = main.shape
    shape = (both // 2, columns)
    outs = [(shape, F32)] + [(shape, BF16)] * (count - 1)
    first, *parts = call(
        functools.partial(shares_kernel, j), outs, [main, rims, after], "vva", flops=BUSY, name="shares"
    )
    return first, parts


def outward_kernel(first_ref, *refs):
    *arrived, out_ref = refs
    total = first_ref[...]
    for piece in arrived:
        total += piece[...].astype(F32)
    out_ref[...] = total.astype(out_ref.dtype)


def outward(first, arrived, dtype):
    operands = [first, *arrived]
    outs = [(first.shape, dtype)]
    return call(outward_kernel, outs, operands, "v" * len(operands), name="outward")[0]


def per_device(flux, footprint, tile_mask, rec_hour, observed, obs_weight, site_count):
    hours, own = flux.shape
    rows, lags, cells = footprint.shape
    devices = cells // own
    far = devices // 2
    near = range(2, far, 2)

    low = flux.astype(BF16)
    far_low = swap(low, far)
    foot = footprint.reshape(rows * lags, cells)
    blocks = tile_mask.shape[0]
    head = blocks * 3 // 8
    top = prepare(foot, tile_mask, low, devices, 0, head)
    ends = tails(low, far_low, top)
    first = window(low, far_low, turn(ends, 1), ends)
    parts = [swap(first, k) for k in near]
    other_first = swap(first, 1)
    bottom = prepare(foot, tile_mask, first, devices, head, blocks - head)
    select, lines = choose(
        rec_hour.reshape(1, rows),
        observed.reshape(1, rows),
        obs_weight.reshape(1, rows),
        site_count,
        first,
        lags,
        hours,
    )
    rest = pack(parts, lines, bottom)
    masked = (top, bottom)
    begun = score(first, rest, masked)
    mism, spread, other, other_rims = adjoint(
        other_first, swap(rest, 1), masked, begun, select, lines, lags
    )

    came_rims = swap(other_rims, 1)
    own_part, own_rims = mine_part(spread, masked)
    rims = join_rims(own_rims, came_rims)
    came = swap(gate(other, rims), 1)
    back = turn(rims, -1)
    main = join(own_part, came, rims)
    far_sum, parts = shares(main, back, 1, rims)
    passed = [swap(part, k) for part, k in zip(parts, near)]
    near_sum, others = shares(main, back, 0, parts[0])
    arrived = [swap(part, k) for part, k in zip(others, near)]
    mism = narrow(mism, far_sum, rows)
    relay = outward(far_sum, passed, BF16)
    total = outward(near_sum, arrived, F32)
    gradient = total + swap(relay, far).astype(F32)
    return (gradient, mism.reshape(rows))


def solution(mesh):
    placed = (
        P("hour", "rcpt"),
        P(("hour", "rcpt"), None, None),
        P(("hour", "rcpt"), None, None),
        P(("hour", "rcpt")),
        P(("hour", "rcpt")),
        P(("hour", "rcpt")),
        P(("hour", "rcpt")),
    )
    return jax.shard_map(
        per_device,
        mesh=mesh,
        in_specs=placed,
        out_specs=(P("hour", "rcpt"), P(("hour", "rcpt"))),
        check_vma=False,
    )
```

```python
import functools

import jax
import jax.numpy as jnp
from jax import lax
from jax.experimental import pallas as pl
from jax.experimental.pallas import tpu as pltpu
from jax.sharding import PartitionSpec as P

RIM = 8
PAIR = 2 * RIM
F32 = jnp.float32
BF16 = jnp.bfloat16
VMEM_LIMIT = 44 * 1024 * 1024
SMALL_LIMIT = 8 * 1024 * 1024
BUSY = 10**10


def swap(block, bit):
    devices = range(lax.axis_size("rcpt"))
    return lax.ppermute(block, "rcpt", [(i, i ^ bit) for i in devices])


def turn(block, distance):
    size = lax.axis_size("hour")
    return lax.ppermute(block, "hour", [(i, (i + distance) % size) for i in range(size)])


def expander(rows, lags, dtype):
    shape = (rows, rows * lags)
    row = lax.broadcasted_iota(jnp.int32, shape, 0)
    column = lax.broadcasted_iota(jnp.int32, shape, 1)
    first = row * lags
    return ((column >= first) & (column < first + lags)).astype(dtype)


def call(kernel, outs, operands, spaces, scratch=(), limit=SMALL_LIMIT, flops=0, moved=0, name=None):
    where = {"v": pltpu.VMEM, "s": pltpu.SMEM, "a": pl.ANY}
    vmem = pl.BlockSpec(memory_space=pltpu.VMEM)
    return pl.pallas_call(
        kernel,
        in_specs=[pl.BlockSpec(memory_space=where[c]) for c in spaces],
        out_specs=[vmem] * len(outs),
        out_shape=[jax.ShapeDtypeStruct(shape, dtype) for shape, dtype in outs],
        scratch_shapes=scratch,
        compiler_params=pltpu.CompilerParams(vmem_limit_bytes=limit),
        cost_estimate=pl.CostEstimate(flops=flops, bytes_accessed=moved, transcendentals=0),
        name=name,
    )(*operands)


def masks_kernel(mask_ref, after_ref, out_ref):
    del after_ref
    mask = mask_ref[...].astype(F32)
    blocks, lags, tiles = mask.shape
    twice = jnp.broadcast_to(mask[:, None], (blocks, 2, lags, tiles))
    out_ref[...] = twice.reshape(blocks, 2 * lags, tiles)


def masks_of(mask, after):
    blocks, lags, tiles = mask.shape
    outs = [((blocks, 2 * lags, tiles), F32)]
    return call(masks_kernel, outs, [mask, after], "va", flops=BUSY, name="masks")[0]


def prepare_kernel(devices, first, foot_hbm, mask_ref, after_ref, masked_ref, foot_ref, sems):
    del after_ref
    me = lax.axis_index("rcpt")
    blocks, group, tiles = mask_ref.shape
    depth, cells = foot_ref.shape
    own = cells // devices
    tile = cells // tiles
    part = foot_hbm.shape[0] // blocks
    used = depth // part
    copies = []
    for b in range(used):
        source = foot_hbm.at[pl.ds((first + b) * part, part)]
        copies.append(pltpu.make_async_copy(source, foot_ref.at[pl.ds(b * part, part)], sems.at[b]))
    for copy in copies:
        copy.start()
    twice = mask_ref[first : first + used].reshape(used * group, tiles)
    wide = jnp.dot(twice.astype(BF16), expander(tiles, tile, BF16), preferred_element_type=F32)
    wide = wide.astype(BF16)
    for b in range(used):
        copies[b].wait()
        for d in range(devices):
            cut = slice(d * own, (d + 1) * own)
            keep = wide[b * group : (b + 1) * group, cut]
            for j in range(part // group):
                at = pl.ds(b * part + j * group, group)
                masked_ref[me ^ d, at, :] = foot_ref[at, cut] * keep


def prepare(foot, mask, after, devices, first, blocks):
    depth, cells = foot.shape
    depth = depth // mask.shape[0] * blocks
    return call(
        functools.partial(prepare_kernel, devices, first),
        [((devices, depth, cells // devices), BF16)],
        [foot, mask, after],
        "ava",
        [pltpu.VMEM((depth, cells), BF16), pltpu.SemaphoreType.DMA((blocks,))],
        limit=VMEM_LIMIT,
        flops=BUSY,
        moved=4 * depth * cells,
        name="prepare",
    )[0]


def choose_kernel(lags, hours, hour_ref, obs_ref, weight_ref, count_ref, after_ref, select_ref, line_ref):
    del after_ref
    rows = hour_ref.shape[1]
    live = (lax.broadcasted_iota(jnp.int32, (1, rows), 1) < count_ref[0]).astype(F32)
    sides = [live * weight_ref[...], obs_ref[...], hour_ref[...].astype(F32)]
    sides = jnp.concatenate([jnp.broadcast_to(side, (8, rows)) for side in sides], axis=0)
    wide = jnp.dot(
        sides,
        expander(rows, lags, F32),
        precision=lax.Precision.HIGHEST,
        preferred_element_type=F32,
    )
    line_ref[...] = wide[: 2 * 8]
    column = lax.broadcasted_iota(jnp.int32, (1, rows * lags), 1)
    hour = wide[2 * 8 : 2 * 8 + 1].astype(jnp.int32) - lax.rem(column, lags)
    slot = jnp.where(hour >= 0, hour, hour + (hours + RIM))
    wanted = lax.broadcasted_iota(jnp.int32, select_ref.shape, 0)
    select_ref[...] = (wanted == slot).astype(F32)


def choose(hour, obs, weight, count, after, lags, hours):
    rows = hour.shape[1]
    return call(
        functools.partial(choose_kernel, lags, hours),
        [((hours + PAIR, rows * lags), F32), ((2 * 8, rows * lags), F32)],
        [hour, obs, weight, count, after],
        "vvvsa",
        flops=BUSY,
        name="choose",
    )


def edge_kernel(low_ref, out_ref):
    hours = low_ref.shape[0]
    out_ref[...] = low_ref[hours - PAIR :].astype(F32)[RIM:].astype(BF16)


def edge(low):
    outs = [((RIM, low.shape[1]), BF16)]
    return call(edge_kernel, outs, [low], "v", name="edge")[0]


def block_kernel(low_ref, rim_ref, after_ref, out_ref):
    del after_ref
    hours = low_ref.shape[0]
    inside = (lax.axis_index("hour") > 0).astype(F32)
    rim = rim_ref[...].astype(F32) * inside
    out_ref[:hours] = low_ref[...]
    out_ref[hours:] = jnp.concatenate([rim, jnp.zeros_like(rim)], axis=0).astype(BF16)


def block_of(low, rim, after):
    hours, columns = low.shape
    outs = [((hours + PAIR, columns), BF16)]
    return call(block_kernel, outs, [low, rim, after], "vva", name="block")[0]


def window_kernel(near_ref, far_ref, after_ref, out_ref):
    del after_ref
    hours = near_ref.shape[0] - PAIR
    out_ref[:hours] = near_ref[:hours]
    out_ref[hours : 2 * hours] = far_ref[:hours]
    rims = [ref[hours:].astype(F32)[:RIM] for ref in (near_ref, far_ref)]
    out_ref[2 * hours :] = jnp.concatenate(rims, axis=0).astype(BF16)


def window(near, far, after):
    height, columns = near.shape
    outs = [((2 * height - PAIR, columns), BF16)]
    return call(window_kernel, outs, [near, far, after], "vva", name="window")[0]


def pack_kernel(count, *refs):
    parts, out_ref = refs[:count], refs[-1]
    height = parts[0].shape[0]
    for i, part in enumerate(parts):
        out_ref[i * height : (i + 1) * height] = part[...]


def pack(parts, *after):
    height, columns = parts[0].shape
    outs = [((len(parts) * height, columns), BF16)]
    spaces = "v" * len(parts) + "a" * len(after)
    kernel = functools.partial(pack_kernel, len(parts))
    return call(kernel, outs, [*parts, *after], spaces, name="pack")[0]


def row_spans(masked_refs):
    spans, at = [], 0
    for masked_ref in masked_refs:
        spans.append(slice(at, at + masked_ref.shape[1]))
        at += masked_ref.shape[1]
    return spans


def add_scores(windows, masked_refs, start, score_ref, window_ref):
    hours = window_ref.shape[0] - PAIR
    half = masked_refs[0].shape[0] // 2
    spans = row_spans(masked_refs)
    for i, read in enumerate(windows):
        rims = read(slice(2 * hours, 2 * hours + PAIR)).astype(F32)
        gap = jnp.zeros_like(rims[:RIM])
        for j in range(2):
            window_ref[:hours] = read(slice(j * hours, (j + 1) * hours))
            rim = rims[j * RIM : (j + 1) * RIM]
            window_ref[hours:] = jnp.concatenate([rim, gap], axis=0).astype(BF16)
            k = (j * half + 2 * i) ^ start
            dims = (((1,), (1,)), ((), ()))
            for at, masked_ref in zip(spans, masked_refs):
                term = lax.dot_general(
                    window_ref[...], masked_ref[k], dims, preferred_element_type=F32
                )
                if start == 0 and i == 0 and j == 0:
                    score_ref[:, at] = term
                else:
                    score_ref[:, at] += term


def readers(first_ref, rest_ref):
    height = first_ref.shape[0]

    def read(i, rows):
        if i == 0:
            return first_ref[rows]
        return rest_ref[(i - 1) * height + rows.start : (i - 1) * height + rows.stop]

    count = 1 + rest_ref.shape[0] // height
    return [functools.partial(read, i) for i in range(count)]


def score_kernel(first_ref, rest_ref, top_ref, low_ref, score_ref, window_ref):
    add_scores(readers(first_ref, rest_ref), (top_ref, low_ref), 0, score_ref, window_ref)


def score(first, rest, masked):
    devices, _, own = masked[0].shape
    depth = sum(part.shape[1] for part in masked)
    width = first.shape[0] // 2 - RIM + PAIR
    return call(
        score_kernel,
        [((width, depth), F32)],
        [first, rest, *masked],
        "vvvv",
        [pltpu.VMEM((width, own), BF16)],
        flops=width * depth * own * devices,
        moved=depth * own * devices,
        name="score",
    )[0]


def terms(spread_ref, masked_refs, k):
    total = None
    for at, masked_ref in zip(row_spans(masked_refs), masked_refs):
        term = jnp.dot(spread_ref[:, at], masked_ref[k], preferred_element_type=F32)
        total = term if total is None else total + term
    return total


def group_sums(values, lags):
    lane = lax.broadcasted_iota(jnp.int32, values.shape, 1)
    size = values.shape[1]
    step = 1
    while step < lags:
        up, down = pltpu.roll(values, step, 1), pltpu.roll(values, size - step, 1)
        values = values + jnp.where((lane & step) != 0, up, down)
        step *= 2
    return values


def adjoint_kernel(
    lags, first_ref, rest_ref, top_ref, low_ref, begun_ref, select_ref, line_ref,
    mism_ref, spread_ref, other_ref, rims_ref, score_ref, window_ref,
):
    width, depth = score_ref.shape
    hours = other_ref.shape[1]
    score_ref[...] = begun_ref[...]
    add_scores(readers(first_ref, rest_ref), (top_ref, low_ref), 1, score_ref, window_ref)
    line = jnp.sum(score_ref[...] * select_ref[...], axis=0, keepdims=True)
    model = group_sums(jnp.broadcast_to(line, (8, depth)), lags)
    mism = line_ref[:8] * (model - line_ref[8:])
    mism_ref[...] = mism
    weighted = mism.astype(BF16).astype(F32)
    for i in range(0, width, PAIR):
        rows = [select_ref[i + j : i + j + 8] * weighted for j in (0, 8)]
        spread_ref[i : i + PAIR] = jnp.concatenate(rows, axis=0).astype(BF16)
    count = top_ref.shape[0] // 4
    for i in range(count):
        edges = []
        for k in (i, i + count):
            term = terms(spread_ref, (top_ref, low_ref), 2 * k + 1)
            other_ref[k] = term[:hours].astype(BF16)
            edges.append(term[hours : hours + RIM])
        rims_ref[i * PAIR : (i + 1) * PAIR] = jnp.concatenate(edges, axis=0).astype(BF16)


def adjoint(first, rest, masked, begun, select, lines, lags):
    devices, _, own = masked[0].shape
    depth = sum(part.shape[1] for part in masked)
    width = begun.shape[0]
    return call(
        functools.partial(adjoint_kernel, lags),
        [
            ((8, depth), F32),
            ((width, depth), BF16),
            ((devices // 2, width - PAIR, own), BF16),
            ((devices // 4 * PAIR, own), BF16),
        ],
        [first, rest, *masked, begun, select, lines],
        "v" * 7,
        [pltpu.VMEM((width, depth), F32), pltpu.VMEM((width, own), BF16)],
        flops=2 * width * depth * own * devices,
        moved=depth * own * devices,
        name="adjoint",
    )


def mine_kernel(spread_ref, top_ref, low_ref, own_ref, rims_ref):
    count = top_ref.shape[0] // 4
    hours = own_ref.shape[1]
    for i in range(count):
        edges = []
        for k in (i, i + count):
            term = terms(spread_ref, (top_ref, low_ref), 2 * k)
            own_ref[k] = term[:hours]
            edges.append(term[hours : hours + RIM])
        rims_ref[i * PAIR : (i + 1) * PAIR] = jnp.concatenate(edges, axis=0)


def mine_part(spread, masked):
    devices, _, own = masked[0].shape
    depth = sum(part.shape[1] for part in masked)
    width = spread.shape[0]
    return call(
        mine_kernel,
        [((devices // 2, width - PAIR, own), F32), ((devices // 4 * PAIR, own), F32)],
        [spread, *masked],
        "vvv",
        flops=width * depth * own * devices,
        moved=depth * own * devices,
        name="mine",
    )


def narrow_kernel(mism_ref, after_ref, out_ref):
    del after_ref
    rows, depth = out_ref.shape[1], mism_ref.shape[1]
    row, column = (lax.broadcasted_iota(jnp.int32, (rows, depth), i) for i in range(2))
    first = (column == row * (depth // rows)).astype(F32)
    narrow = lax.dot_general(
        mism_ref[...],
        first,
        (((1,), (1,)), ((), ())),
        precision=lax.Precision.HIGHEST,
        preferred_element_type=F32,
    )
    out_ref[...] = narrow[:1]


def narrow(mism, after, rows):
    outs = [((1, rows), F32)]
    return call(narrow_kernel, outs, [mism, after], "va", flops=BUSY, name="narrow")[0]


def gate_kernel(rows_ref, after_ref, out_ref):
    del after_ref
    out_ref[...] = rows_ref[...]


def gate(rows, after):
    outs = [(rows.shape, rows.dtype)]
    return call(gate_kernel, outs, [rows, after], "va", name="gate")[0]


def join_rims_kernel(own_ref, came_ref, out_ref):
    out_ref[...] = (own_ref[...] + came_ref[...].astype(F32)).astype(BF16)


def join_rims(own, came):
    return call(join_rims_kernel, [(own.shape, BF16)], [own, came], "vv", name="rims")[0]


def join_kernel(own_ref, came_ref, after_ref, main_ref):
    del after_ref
    half, hours, _ = own_ref.shape
    for i in range(half // 2):
        for j in range(2):
            k = i + j * (half // 2)
            main_ref[i, j * hours : (j + 1) * hours] = own_ref[k] + came_ref[k].astype(F32)


def join(own, came, after):
    half, hours, columns = own.shape
    outs = [((half // 2, 2 * hours, columns), F32)]
    return call(join_kernel, outs, [own, came, after], "vva", flops=BUSY, name="join")[0]


def with_rims(main_ref, rims_ref, i, j):
    hours = main_ref.shape[1] // 2
    inside = (lax.axis_index("hour") < lax.axis_size("hour") - 1).astype(F32)
    rims = rims_ref[i * PAIR : (i + 1) * PAIR].astype(F32) * inside
    at = (j + 1) * hours - RIM
    last = main_ref[i, at : at + RIM] + rims[j * RIM : (j + 1) * RIM]
    return jnp.concatenate([main_ref[i, j * hours : at], last], axis=0)


def shares_kernel(j, main_ref, rims_ref, after_ref, first_ref, *outs):
    del after_ref
    first_ref[...] = with_rims(main_ref, rims_ref, 0, j)
    for i, out in enumerate(outs):
        out[...] = with_rims(main_ref, rims_ref, i + 1, j).astype(BF16)


def shares(main, rims, j, after):
    count, both, columns = main.shape
    shape = (both // 2, columns)
    outs = [(shape, F32)] + [(shape, BF16)] * (count - 1)
    first, *parts = call(
        functools.partial(shares_kernel, j), outs, [main, rims, after], "vva", flops=BUSY, name="shares"
    )
    return first, parts


def outward_kernel(first_ref, *refs):
    *arrived, out_ref = refs
    total = first_ref[...]
    for piece in arrived:
        total += piece[...].astype(F32)
    out_ref[...] = total.astype(out_ref.dtype)


def outward(first, arrived, dtype):
    operands = [first, *arrived]
    outs = [(first.shape, dtype)]
    return call(outward_kernel, outs, operands, "v" * len(operands), name="outward")[0]


def per_device(flux, footprint, tile_mask, rec_hour, observed, obs_weight, site_count):
    hours, own = flux.shape
    rows, lags, cells = footprint.shape
    devices = cells // own
    far = devices // 2
    near = range(2, far, 2)

    low = flux.astype(BF16)
    end = edge(low)
    masks = masks_of(tile_mask, end)
    block = block_of(low, turn(end, 1), masks)
    far_block = swap(block, far)
    foot = footprint.reshape(rows * lags, cells)
    blocks = tile_mask.shape[0]
    head = blocks * 3 // 8
    top = prepare(foot, masks, block, devices, 0, head)
    first = window(block, far_block, top)
    parts = [swap(first, k) for k in near]
    other_first = swap(first, 1)
    bottom = prepare(foot, masks, first, devices, head, blocks - head)
    select, lines = choose(
        rec_hour.reshape(1, rows),
        observed.reshape(1, rows),
        obs_weight.reshape(1, rows),
        site_count,
        first,
        lags,
        hours,
    )
    rest = pack(parts, lines, bottom)
    masked = (top, bottom)
    begun = score(first, rest, masked)
    mism, spread, other, other_rims = adjoint(
        other_first, swap(rest, 1), masked, begun, select, lines, lags
    )

    came_rims = swap(other_rims, 1)
    own_part, own_rims = mine_part(spread, masked)
    rims = join_rims(own_rims, came_rims)
    came = swap(gate(other, rims), 1)
    back = turn(rims, -1)
    main = join(own_part, came, rims)
    far_sum, parts = shares(main, back, 1, rims)
    passed = [swap(part, k) for part, k in zip(parts, near)]
    near_sum, others = shares(main, back, 0, parts[0])
    arrived = [swap(part, k) for part, k in zip(others, near)]
    mism = narrow(mism, far_sum, rows)
    relay = outward(far_sum, passed, BF16)
    total = outward(near_sum, arrived, F32)
    gradient = total + swap(relay, far).astype(F32)
    return (gradient, mism.reshape(rows))


def solution(mesh):
    placed = (
        P("hour", "rcpt"),
        P(("hour", "rcpt"), None, None),
        P(("hour", "rcpt"), None, None),
        P(("hour", "rcpt")),
        P(("hour", "rcpt")),
        P(("hour", "rcpt")),
        P(("hour", "rcpt")),
    )
    return jax.shard_map(
        per_device,
        mesh=mesh,
        in_specs=placed,
        out_specs=(P("hour", "rcpt"), P(("hour", "rcpt"))),
        check_vma=False,
    )
```

```python
import functools

import jax
import jax.numpy as jnp
from jax import lax
from jax.experimental import pallas as pl
from jax.experimental.pallas import tpu as pltpu
from jax.sharding import PartitionSpec as P

RIM = 8
PAIR = 2 * RIM
F32 = jnp.float32
BF16 = jnp.bfloat16
VMEM_LIMIT = 44 * 1024 * 1024
SMALL_LIMIT = 8 * 1024 * 1024
BUSY = 10**10


def swap(block, bit):
    devices = range(lax.axis_size("rcpt"))
    return lax.ppermute(block, "rcpt", [(i, i ^ bit) for i in devices])


def turn(block, distance):
    size = lax.axis_size("hour")
    return lax.ppermute(block, "hour", [(i, (i + distance) % size) for i in range(size)])


def expander(rows, lags, dtype):
    shape = (rows, rows * lags)
    row = lax.broadcasted_iota(jnp.int32, shape, 0)
    column = lax.broadcasted_iota(jnp.int32, shape, 1)
    first = row * lags
    return ((column >= first) & (column < first + lags)).astype(dtype)


def call(kernel, outs, operands, spaces, scratch=(), limit=SMALL_LIMIT, flops=0, moved=0, name=None):
    where = {"v": pltpu.VMEM, "s": pltpu.SMEM, "a": pl.ANY}
    vmem = pl.BlockSpec(memory_space=pltpu.VMEM)
    return pl.pallas_call(
        kernel,
        in_specs=[pl.BlockSpec(memory_space=where[c]) for c in spaces],
        out_specs=[vmem] * len(outs),
        out_shape=[jax.ShapeDtypeStruct(shape, dtype) for shape, dtype in outs],
        scratch_shapes=scratch,
        compiler_params=pltpu.CompilerParams(vmem_limit_bytes=limit),
        cost_estimate=pl.CostEstimate(flops=flops, bytes_accessed=moved, transcendentals=0),
        name=name,
    )(*operands)


def masks_kernel(mask_ref, after_ref, out_ref):
    del after_ref
    mask = mask_ref[...].astype(F32)
    blocks, lags, tiles = mask.shape
    twice = jnp.broadcast_to(mask[:, None], (blocks, 2, lags, tiles))
    out_ref[...] = twice.reshape(blocks, 2 * lags, tiles)


def masks_of(mask, after):
    blocks, lags, tiles = mask.shape
    outs = [((blocks, 2 * lags, tiles), F32)]
    return call(masks_kernel, outs, [mask, after], "va", flops=BUSY, name="masks")[0]


def prepare_kernel(devices, first, foot_hbm, mask_ref, after_ref, masked_ref, foot_ref, sems):
    del after_ref
    me = lax.axis_index("rcpt")
    blocks, group, tiles = mask_ref.shape
    depth, cells = foot_ref.shape
    own = cells // devices
    tile = cells // tiles
    part = foot_hbm.shape[0] // blocks
    used = depth // part
    copies = []
    for b in range(used):
        source = foot_hbm.at[pl.ds((first + b) * part, part)]
        copies.append(pltpu.make_async_copy(source, foot_ref.at[pl.ds(b * part, part)], sems.at[b]))
    for copy in copies:
        copy.start()
    twice = mask_ref[first : first + used].reshape(used * group, tiles)
    wide = jnp.dot(twice.astype(BF16), expander(tiles, tile, BF16), preferred_element_type=F32)
    wide = wide.astype(BF16)
    for b in range(used):
        copies[b].wait()
        for d in range(devices):
            cut = slice(d * own, (d + 1) * own)
            keep = wide[b * group : (b + 1) * group, cut]
            for j in range(part // group):
                at = pl.ds(b * part + j * group, group)
                masked_ref[me ^ d, at, :] = foot_ref[at, cut] * keep


def prepare(foot, mask, after, devices, first, blocks):
    depth, cells = foot.shape
    depth = depth // mask.shape[0] * blocks
    return call(
        functools.partial(prepare_kernel, devices, first),
        [((devices, depth, cells // devices), BF16)],
        [foot, mask, after],
        "ava",
        [pltpu.VMEM((depth, cells), BF16), pltpu.SemaphoreType.DMA((blocks,))],
        limit=VMEM_LIMIT,
        flops=BUSY,
        moved=4 * depth * cells,
        name="prepare",
    )[0]


def choose_kernel(lags, hours, hour_ref, obs_ref, weight_ref, count_ref, after_ref, select_ref, line_ref):
    del after_ref
    rows = hour_ref.shape[1]
    live = (lax.broadcasted_iota(jnp.int32, (1, rows), 1) < count_ref[0]).astype(F32)
    sides = [live * weight_ref[...], obs_ref[...], hour_ref[...].astype(F32)]
    sides = jnp.concatenate([jnp.broadcast_to(side, (8, rows)) for side in sides], axis=0)
    wide = jnp.dot(
        sides,
        expander(rows, lags, F32),
        precision=lax.Precision.HIGHEST,
        preferred_element_type=F32,
    )
    line_ref[...] = wide[: 2 * 8]
    column = lax.broadcasted_iota(jnp.int32, (1, rows * lags), 1)
    hour = wide[2 * 8 : 2 * 8 + 1].astype(jnp.int32) - lax.rem(column, lags)
    slot = jnp.where(hour >= 0, hour, hour + (hours + RIM))
    wanted = lax.broadcasted_iota(jnp.int32, select_ref.shape, 0)
    select_ref[...] = (wanted == slot).astype(F32)


def choose(hour, obs, weight, count, after, lags, hours):
    rows = hour.shape[1]
    return call(
        functools.partial(choose_kernel, lags, hours),
        [((hours + PAIR, rows * lags), F32), ((2 * 8, rows * lags), F32)],
        [hour, obs, weight, count, after],
        "vvvsa",
        flops=BUSY,
        name="choose",
    )


def edge_kernel(low_ref, out_ref):
    hours = low_ref.shape[0]
    out_ref[...] = low_ref[hours - PAIR :].astype(F32)[RIM:].astype(BF16)


def edge(low):
    outs = [((RIM, low.shape[1]), BF16)]
    return call(edge_kernel, outs, [low], "v", name="edge")[0]


def block_kernel(low_ref, rim_ref, after_ref, out_ref):
    del after_ref
    hours = low_ref.shape[0]
    inside = (lax.axis_index("hour") > 0).astype(F32)
    rim = rim_ref[...].astype(F32) * inside
    out_ref[:hours] = low_ref[...]
    out_ref[hours:] = jnp.concatenate([rim, jnp.zeros_like(rim)], axis=0).astype(BF16)


def block_of(low, rim, after):
    hours, columns = low.shape
    outs = [((hours + PAIR, columns), BF16)]
    return call(block_kernel, outs, [low, rim, after], "vva", name="block")[0]


def window_kernel(near_ref, far_ref, after_ref, out_ref):
    del after_ref
    hours = near_ref.shape[0] - PAIR
    out_ref[:hours] = near_ref[:hours]
    out_ref[hours : 2 * hours] = far_ref[:hours]
    rims = [ref[hours:].astype(F32)[:RIM] for ref in (near_ref, far_ref)]
    out_ref[2 * hours :] = jnp.concatenate(rims, axis=0).astype(BF16)


def window(near, far, after):
    height, columns = near.shape
    outs = [((2 * height - PAIR, columns), BF16)]
    return call(window_kernel, outs, [near, far, after], "vva", name="window")[0]


def pack_kernel(count, *refs):
    parts, out_ref = refs[:count], refs[-1]
    height = parts[0].shape[0]
    for i, part in enumerate(parts):
        out_ref[i * height : (i + 1) * height] = part[...]


def pack(parts, *after):
    height, columns = parts[0].shape
    outs = [((len(parts) * height, columns), BF16)]
    spaces = "v" * len(parts) + "a" * len(after)
    kernel = functools.partial(pack_kernel, len(parts))
    return call(kernel, outs, [*parts, *after], spaces, name="pack")[0]


def row_spans(masked_refs):
    spans, at = [], 0
    for masked_ref in masked_refs:
        spans.append(slice(at, at + masked_ref.shape[1]))
        at += masked_ref.shape[1]
    return spans


def add_scores(windows, masked_refs, start, score_ref, window_ref):
    hours = window_ref.shape[0] - PAIR
    half = masked_refs[0].shape[0] // 2
    spans = row_spans(masked_refs)
    for i, read in enumerate(windows):
        rims = read(slice(2 * hours, 2 * hours + PAIR)).astype(F32)
        gap = jnp.zeros_like(rims[:RIM])
        for j in range(2):
            window_ref[:hours] = read(slice(j * hours, (j + 1) * hours))
            rim = rims[j * RIM : (j + 1) * RIM]
            window_ref[hours:] = jnp.concatenate([rim, gap], axis=0).astype(BF16)
            k = (j * half + 2 * i) ^ start
            dims = (((1,), (1,)), ((), ()))
            for at, masked_ref in zip(spans, masked_refs):
                term = lax.dot_general(
                    window_ref[...], masked_ref[k], dims, preferred_element_type=F32
                )
                if start == 0 and i == 0 and j == 0:
                    score_ref[:, at] = term
                else:
                    score_ref[:, at] += term


def readers(rest_ref, height):
    def read(i, rows):
        return rest_ref[i * height + rows.start : i * height + rows.stop]

    return [functools.partial(read, i) for i in range(rest_ref.shape[0] // height)]


def score_kernel(rest_ref, top_ref, low_ref, score_ref, window_ref):
    height = 2 * window_ref.shape[0] - PAIR
    add_scores(readers(rest_ref, height), (top_ref, low_ref), 0, score_ref, window_ref)


def score(rest, masked):
    devices, _, own = masked[0].shape
    depth = sum(part.shape[1] for part in masked)
    width = rest.shape[0] // (devices // 4) // 2 - RIM + PAIR
    return call(
        score_kernel,
        [((width, depth), F32)],
        [rest, *masked],
        "vvv",
        [pltpu.VMEM((width, own), BF16)],
        flops=width * depth * own * devices,
        moved=depth * own * devices,
        name="score",
    )[0]


def terms(spread_ref, masked_refs, k):
    total = None
    for at, masked_ref in zip(row_spans(masked_refs), masked_refs):
        term = jnp.dot(spread_ref[:, at], masked_ref[k], preferred_element_type=F32)
        total = term if total is None else total + term
    return total


def group_sums(values, lags):
    lane = lax.broadcasted_iota(jnp.int32, values.shape, 1)
    size = values.shape[1]
    step = 1
    while step < lags:
        up, down = pltpu.roll(values, step, 1), pltpu.roll(values, size - step, 1)
        values = values + jnp.where((lane & step) != 0, up, down)
        step *= 2
    return values


def adjoint_kernel(
    lags, rest_ref, top_ref, low_ref, begun_ref, select_ref, line_ref,
    mism_ref, spread_ref, other_ref, rims_ref, score_ref, window_ref,
):
    width, depth = score_ref.shape
    hours = other_ref.shape[1]
    score_ref[...] = begun_ref[...]
    height = 2 * window_ref.shape[0] - PAIR
    add_scores(readers(rest_ref, height), (top_ref, low_ref), 1, score_ref, window_ref)
    line = jnp.sum(score_ref[...] * select_ref[...], axis=0, keepdims=True)
    model = group_sums(jnp.broadcast_to(line, (8, depth)), lags)
    mism = line_ref[:8] * (model - line_ref[8:])
    mism_ref[...] = mism
    weighted = mism.astype(BF16).astype(F32)
    for i in range(0, width, PAIR):
        rows = [select_ref[i + j : i + j + 8] * weighted for j in (0, 8)]
        spread_ref[i : i + PAIR] = jnp.concatenate(rows, axis=0).astype(BF16)
    count = top_ref.shape[0] // 4
    for i in range(count):
        edges = []
        for k in (i, i + count):
            term = terms(spread_ref, (top_ref, low_ref), 2 * k + 1)
            other_ref[k] = term[:hours].astype(BF16)
            edges.append(term[hours : hours + RIM])
        rims_ref[i * PAIR : (i + 1) * PAIR] = jnp.concatenate(edges, axis=0).astype(BF16)


def adjoint(rest, masked, begun, select, lines, lags):
    devices, _, own = masked[0].shape
    depth = sum(part.shape[1] for part in masked)
    width = begun.shape[0]
    return call(
        functools.partial(adjoint_kernel, lags),
        [
            ((8, depth), F32),
            ((width, depth), BF16),
            ((devices // 2, width - PAIR, own), BF16),
            ((devices // 4 * PAIR, own), BF16),
        ],
        [rest, *masked, begun, select, lines],
        "v" * 6,
        [pltpu.VMEM((width, depth), F32), pltpu.VMEM((width, own), BF16)],
        flops=2 * width * depth * own * devices,
        moved=depth * own * devices,
        name="adjoint",
    )


def mine_kernel(spread_ref, top_ref, low_ref, own_ref, rims_ref):
    count = top_ref.shape[0] // 4
    hours = own_ref.shape[1]
    for i in range(count):
        edges = []
        for k in (i, i + count):
            term = terms(spread_ref, (top_ref, low_ref), 2 * k)
            own_ref[k] = term[:hours]
            edges.append(term[hours : hours + RIM])
        rims_ref[i * PAIR : (i + 1) * PAIR] = jnp.concatenate(edges, axis=0)


def mine_part(spread, masked):
    devices, _, own = masked[0].shape
    depth = sum(part.shape[1] for part in masked)
    width = spread.shape[0]
    return call(
        mine_kernel,
        [((devices // 2, width - PAIR, own), F32), ((devices // 4 * PAIR, own), F32)],
        [spread, *masked],
        "vvv",
        flops=width * depth * own * devices,
        moved=depth * own * devices,
        name="mine",
    )


def narrow_kernel(mism_ref, after_ref, out_ref):
    del after_ref
    rows, depth = out_ref.shape[1], mism_ref.shape[1]
    row, column = (lax.broadcasted_iota(jnp.int32, (rows, depth), i) for i in range(2))
    first = (column == row * (depth // rows)).astype(F32)
    narrow = lax.dot_general(
        mism_ref[...],
        first,
        (((1,), (1,)), ((), ())),
        precision=lax.Precision.HIGHEST,
        preferred_element_type=F32,
    )
    out_ref[...] = narrow[:1]


def narrow(mism, after, rows):
    outs = [((1, rows), F32)]
    return call(narrow_kernel, outs, [mism, after], "va", flops=BUSY, name="narrow")[0]


def gate_kernel(rows_ref, after_ref, out_ref):
    del after_ref
    out_ref[...] = rows_ref[...]


def gate(rows, after):
    outs = [(rows.shape, rows.dtype)]
    return call(gate_kernel, outs, [rows, after], "va", name="gate")[0]


def join_rims_kernel(own_ref, came_ref, out_ref):
    out_ref[...] = (own_ref[...] + came_ref[...].astype(F32)).astype(BF16)


def join_rims(own, came):
    return call(join_rims_kernel, [(own.shape, BF16)], [own, came], "vv", name="rims")[0]


def join_kernel(own_ref, came_ref, after_ref, main_ref):
    del after_ref
    half, hours, _ = own_ref.shape
    for i in range(half // 2):
        for j in range(2):
            k = i + j * (half // 2)
            main_ref[i, j * hours : (j + 1) * hours] = own_ref[k] + came_ref[k].astype(F32)


def join(own, came, after):
    half, hours, columns = own.shape
    outs = [((half // 2, 2 * hours, columns), F32)]
    return call(join_kernel, outs, [own, came, after], "vva", flops=BUSY, name="join")[0]


def with_rims(main_ref, rims_ref, i, j):
    hours = main_ref.shape[1] // 2
    inside = (lax.axis_index("hour") < lax.axis_size("hour") - 1).astype(F32)
    rims = rims_ref[i * PAIR : (i + 1) * PAIR].astype(F32) * inside
    at = (j + 1) * hours - RIM
    last = main_ref[i, at : at + RIM] + rims[j * RIM : (j + 1) * RIM]
    return jnp.concatenate([main_ref[i, j * hours : at], last], axis=0)


def shares_kernel(j, main_ref, rims_ref, after_ref, first_ref, *outs):
    del after_ref
    first_ref[...] = with_rims(main_ref, rims_ref, 0, j)
    for i, out in enumerate(outs):
        out[...] = with_rims(main_ref, rims_ref, i + 1, j).astype(BF16)


def shares(main, rims, j, after):
    count, both, columns = main.shape
    shape = (both // 2, columns)
    outs = [(shape, F32)] + [(shape, BF16)] * (count - 1)
    first, *parts = call(
        functools.partial(shares_kernel, j), outs, [main, rims, after], "vva", flops=BUSY, name="shares"
    )
    return first, parts


def outward_kernel(first_ref, *refs):
    *arrived, out_ref = refs
    total = first_ref[...]
    for piece in arrived:
        total += piece[...].astype(F32)
    out_ref[...] = total.astype(out_ref.dtype)


def outward(first, arrived, dtype):
    operands = [first, *arrived]
    outs = [(first.shape, dtype)]
    return call(outward_kernel, outs, operands, "v" * len(operands), name="outward")[0]


def per_device(flux, footprint, tile_mask, rec_hour, observed, obs_weight, site_count):
    hours, own = flux.shape
    rows, lags, cells = footprint.shape
    devices = cells // own
    far = devices // 2
    near = range(2, far, 2)

    low = flux.astype(BF16)
    end = edge(low)
    masks = masks_of(tile_mask, end)
    block = block_of(low, turn(end, 1), masks)
    far_block = swap(block, far)
    foot = footprint.reshape(rows * lags, cells)
    blocks = tile_mask.shape[0]
    head = blocks * 3 // 8
    top = prepare(foot, masks, block, devices, 0, head)
    first = window(block, far_block, top)
    parts = [swap(first, k) for k in near]
    bottom = prepare(foot, masks, first, devices, head, blocks - head)
    select, lines = choose(
        rec_hour.reshape(1, rows),
        observed.reshape(1, rows),
        obs_weight.reshape(1, rows),
        site_count,
        first,
        lags,
        hours,
    )
    rest = pack([first, *parts], lines, bottom)
    masked = (top, bottom)
    begun = score(rest, masked)
    mism, spread, other, other_rims = adjoint(
        swap(rest, 1), masked, begun, select, lines, lags
    )

    came_rims = swap(other_rims, 1)
    own_part, own_rims = mine_part(spread, masked)
    rims = join_rims(own_rims, came_rims)
    came = swap(gate(other, rims), 1)
    back = turn(rims, -1)
    main = join(own_part, came, rims)
    far_sum, parts = shares(main, back, 1, rims)
    passed = [swap(part, k) for part, k in zip(parts, near)]
    near_sum, others = shares(main, back, 0, parts[0])
    arrived = [swap(part, k) for part, k in zip(others, near)]
    mism = narrow(mism, far_sum, rows)
    relay = outward(far_sum, passed, BF16)
    total = outward(near_sum, arrived, F32)
    gradient = total + swap(relay, far).astype(F32)
    return (gradient, mism.reshape(rows))


def solution(mesh):
    placed = (
        P("hour", "rcpt"),
        P(("hour", "rcpt"), None, None),
        P(("hour", "rcpt"), None, None),
        P(("hour", "rcpt")),
        P(("hour", "rcpt")),
        P(("hour", "rcpt")),
        P(("hour", "rcpt")),
    )
    return jax.shard_map(
        per_device,
        mesh=mesh,
        in_specs=placed,
        out_specs=(P("hour", "rcpt"), P(("hour", "rcpt"))),
        check_vma=False,
    )
```

```python
import functools

import jax
import jax.numpy as jnp
from jax import lax
from jax.experimental import pallas as pl
from jax.experimental.pallas import tpu as pltpu
from jax.sharding import PartitionSpec as P

RIM = 8
PAIR = 2 * RIM
F32 = jnp.float32
BF16 = jnp.bfloat16
VMEM_LIMIT = 44 * 1024 * 1024
SMALL_LIMIT = 8 * 1024 * 1024
BUSY = 10**10


def swap(block, bit):
    devices = range(lax.axis_size("rcpt"))
    return lax.ppermute(block, "rcpt", [(i, i ^ bit) for i in devices])


def turn(block, distance):
    size = lax.axis_size("hour")
    return lax.ppermute(block, "hour", [(i, (i + distance) % size) for i in range(size)])


def expander(rows, lags, dtype):
    shape = (rows, rows * lags)
    row = lax.broadcasted_iota(jnp.int32, shape, 0)
    column = lax.broadcasted_iota(jnp.int32, shape, 1)
    first = row * lags
    return ((column >= first) & (column < first + lags)).astype(dtype)


def call(kernel, outs, operands, spaces, scratch=(), limit=SMALL_LIMIT, flops=0, moved=0, name=None):
    where = {"v": pltpu.VMEM, "s": pltpu.SMEM, "a": pl.ANY}
    vmem = pl.BlockSpec(memory_space=pltpu.VMEM)
    return pl.pallas_call(
        kernel,
        in_specs=[pl.BlockSpec(memory_space=where[c]) for c in spaces],
        out_specs=[vmem] * len(outs),
        out_shape=[jax.ShapeDtypeStruct(shape, dtype) for shape, dtype in outs],
        scratch_shapes=scratch,
        compiler_params=pltpu.CompilerParams(vmem_limit_bytes=limit),
        cost_estimate=pl.CostEstimate(flops=flops, bytes_accessed=moved, transcendentals=0),
        name=name,
    )(*operands)


def masks_kernel(mask_ref, after_ref, out_ref):
    del after_ref
    mask = mask_ref[...].astype(F32)
    blocks, lags, tiles = mask.shape
    twice = jnp.broadcast_to(mask[:, None], (blocks, 2, lags, tiles))
    out_ref[...] = twice.reshape(blocks, 2 * lags, tiles)


def masks_of(mask, after):
    blocks, lags, tiles = mask.shape
    outs = [((blocks, 2 * lags, tiles), F32)]
    return call(masks_kernel, outs, [mask, after], "va", flops=BUSY, name="masks")[0]


def prepare_kernel(devices, first, foot_hbm, mask_ref, after_ref, masked_ref, foot_ref, sems):
    del after_ref
    me = lax.axis_index("rcpt")
    blocks, group, tiles = mask_ref.shape
    depth, cells = foot_ref.shape
    own = cells // devices
    tile = cells // tiles
    part = foot_hbm.shape[0] // blocks
    used = depth // part
    copies = []
    for b in range(used):
        source = foot_hbm.at[pl.ds((first + b) * part, part)]
        copies.append(pltpu.make_async_copy(source, foot_ref.at[pl.ds(b * part, part)], sems.at[b]))
    for copy in copies:
        copy.start()
    twice = mask_ref[first : first + used].reshape(used * group, tiles)
    wide = jnp.dot(twice.astype(BF16), expander(tiles, tile, BF16), preferred_element_type=F32)
    wide = wide.astype(BF16)
    for b in range(used):
        copies[b].wait()
        for d in range(devices):
            cut = slice(d * own, (d + 1) * own)
            keep = wide[b * group : (b + 1) * group, cut]
            for j in range(part // group):
                at = pl.ds(b * part + j * group, group)
                masked_ref[me ^ d, at, :] = foot_ref[at, cut] * keep


def prepare(foot, mask, after, devices, first, blocks):
    depth, cells = foot.shape
    depth = depth // mask.shape[0] * blocks
    return call(
        functools.partial(prepare_kernel, devices, first),
        [((devices, depth, cells // devices), BF16)],
        [foot, mask, after],
        "ava",
        [pltpu.VMEM((depth, cells), BF16), pltpu.SemaphoreType.DMA((blocks,))],
        limit=VMEM_LIMIT,
        flops=BUSY,
        moved=4 * depth * cells,
        name="prepare",
    )[0]


def choose_kernel(lags, hours, hour_ref, obs_ref, weight_ref, count_ref, after_ref, select_ref, line_ref):
    del after_ref
    rows = hour_ref.shape[1]
    live = (lax.broadcasted_iota(jnp.int32, (1, rows), 1) < count_ref[0]).astype(F32)
    sides = [live * weight_ref[...], obs_ref[...], hour_ref[...].astype(F32)]
    sides = jnp.concatenate([jnp.broadcast_to(side, (8, rows)) for side in sides], axis=0)
    wide = jnp.dot(
        sides,
        expander(rows, lags, F32),
        precision=lax.Precision.HIGHEST,
        preferred_element_type=F32,
    )
    line_ref[...] = wide[: 2 * 8]
    column = lax.broadcasted_iota(jnp.int32, (1, rows * lags), 1)
    hour = wide[2 * 8 : 2 * 8 + 1].astype(jnp.int32) - lax.rem(column, lags)
    slot = jnp.where(hour >= 0, hour, hour + (hours + RIM))
    wanted = lax.broadcasted_iota(jnp.int32, select_ref.shape, 0)
    select_ref[...] = (wanted == slot).astype(F32)


def choose(hour, obs, weight, count, after, lags, hours):
    rows = hour.shape[1]
    return call(
        functools.partial(choose_kernel, lags, hours),
        [((hours + PAIR, rows * lags), F32), ((2 * 8, rows * lags), F32)],
        [hour, obs, weight, count, after],
        "vvvsa",
        flops=BUSY,
        name="choose",
    )


def edge_kernel(low_ref, out_ref):
    hours = low_ref.shape[0]
    out_ref[...] = low_ref[hours - PAIR :].astype(F32)[RIM:].astype(BF16)


def edge(low):
    outs = [((RIM, low.shape[1]), BF16)]
    return call(edge_kernel, outs, [low], "v", name="edge")[0]


def block_kernel(low_ref, rim_ref, after_ref, out_ref):
    del after_ref
    hours = low_ref.shape[0]
    inside = (lax.axis_index("hour") > 0).astype(F32)
    rim = rim_ref[...].astype(F32) * inside
    out_ref[:hours] = low_ref[...]
    out_ref[hours:] = jnp.concatenate([rim, jnp.zeros_like(rim)], axis=0).astype(BF16)


def block_of(low, rim, after):
    hours, columns = low.shape
    outs = [((hours + PAIR, columns), BF16)]
    return call(block_kernel, outs, [low, rim, after], "vva", name="block")[0]


def window_kernel(near_ref, far_ref, after_ref, out_ref):
    del after_ref
    hours = near_ref.shape[0] - PAIR
    out_ref[:hours] = near_ref[:hours]
    out_ref[hours : 2 * hours] = far_ref[:hours]
    rims = [ref[hours:].astype(F32)[:RIM] for ref in (near_ref, far_ref)]
    out_ref[2 * hours :] = jnp.concatenate(rims, axis=0).astype(BF16)


def window(near, far, after):
    height, columns = near.shape
    outs = [((2 * height - PAIR, columns), BF16)]
    return call(window_kernel, outs, [near, far, after], "vva", name="window")[0]


def pack_kernel(count, *refs):
    parts, out_ref = refs[:count], refs[-1]
    height = parts[0].shape[0]
    for i, part in enumerate(parts):
        out_ref[i * height : (i + 1) * height] = part[...]


def pack(parts, *after):
    height, columns = parts[0].shape
    outs = [((len(parts) * height, columns), BF16)]
    spaces = "v" * len(parts) + "a" * len(after)
    kernel = functools.partial(pack_kernel, len(parts))
    return call(kernel, outs, [*parts, *after], spaces, name="pack")[0]


def row_spans(masked_refs):
    spans, at = [], 0
    for masked_ref in masked_refs:
        spans.append(slice(at, at + masked_ref.shape[1]))
        at += masked_ref.shape[1]
    return spans


def add_scores(windows, masked_refs, start, score_ref, window_ref):
    hours = window_ref.shape[0] - PAIR
    half = masked_refs[0].shape[0] // 2
    spans = row_spans(masked_refs)
    for i, read in enumerate(windows):
        rims = read(slice(2 * hours, 2 * hours + PAIR)).astype(F32)
        gap = jnp.zeros_like(rims[:RIM])
        for j in range(2):
            window_ref[:hours] = read(slice(j * hours, (j + 1) * hours))
            rim = rims[j * RIM : (j + 1) * RIM]
            window_ref[hours:] = jnp.concatenate([rim, gap], axis=0).astype(BF16)
            k = (j * half + 2 * i) ^ start
            dims = (((1,), (1,)), ((), ()))
            for at, masked_ref in zip(spans, masked_refs):
                term = lax.dot_general(
                    window_ref[...], masked_ref[k], dims, preferred_element_type=F32
                )
                if start == 0 and i == 0 and j == 0:
                    score_ref[:, at] = term
                else:
                    score_ref[:, at] += term


def readers(rest_ref, height):
    def read(i, rows):
        return rest_ref[i * height + rows.start : i * height + rows.stop]

    return [functools.partial(read, i) for i in range(rest_ref.shape[0] // height)]


def score_kernel(rest_ref, top_ref, low_ref, score_ref, window_ref):
    height = 2 * window_ref.shape[0] - PAIR
    add_scores(readers(rest_ref, height), (top_ref, low_ref), 0, score_ref, window_ref)


def score(rest, masked):
    devices, _, own = masked[0].shape
    depth = sum(part.shape[1] for part in masked)
    width = rest.shape[0] // (devices // 4) // 2 - RIM + PAIR
    return call(
        score_kernel,
        [((width, depth), F32)],
        [rest, *masked],
        "vvv",
        [pltpu.VMEM((width, own), BF16)],
        flops=width * depth * own * devices,
        moved=depth * own * devices,
        name="score",
    )[0]


def terms(spread_ref, masked_refs, k):
    total = None
    for at, masked_ref in zip(row_spans(masked_refs), masked_refs):
        term = jnp.dot(spread_ref[:, at], masked_ref[k], preferred_element_type=F32)
        total = term if total is None else total + term
    return total


def group_sums(values, lags):
    lane = lax.broadcasted_iota(jnp.int32, values.shape, 1)
    size = values.shape[1]
    step = 1
    while step < lags:
        up, down = pltpu.roll(values, step, 1), pltpu.roll(values, size - step, 1)
        values = values + jnp.where((lane & step) != 0, up, down)
        step *= 2
    return values


def adjoint_kernel(
    lags, rest_ref, top_ref, low_ref, begun_ref, select_ref, line_ref,
    mism_ref, spread_ref, other_ref, rims_ref, score_ref, window_ref,
):
    width, depth = score_ref.shape
    hours = other_ref.shape[1]
    score_ref[...] = begun_ref[...]
    height = 2 * window_ref.shape[0] - PAIR
    add_scores(readers(rest_ref, height), (top_ref, low_ref), 1, score_ref, window_ref)
    line = jnp.sum(score_ref[...] * select_ref[...], axis=0, keepdims=True)
    model = group_sums(jnp.broadcast_to(line, (8, depth)), lags)
    mism = line_ref[:8] * (model - line_ref[8:])
    mism_ref[...] = mism
    weighted = mism.astype(BF16).astype(F32)
    for i in range(0, width, PAIR):
        rows = [select_ref[i + j : i + j + 8] * weighted for j in (0, 8)]
        spread_ref[i : i + PAIR] = jnp.concatenate(rows, axis=0).astype(BF16)
    count = top_ref.shape[0] // 4
    for i in range(count):
        edges = []
        for k in (i, i + count):
            term = terms(spread_ref, (top_ref, low_ref), 2 * k + 1)
            other_ref[k] = term[:hours].astype(BF16)
            edges.append(term[hours : hours + RIM])
        rims_ref[i * PAIR : (i + 1) * PAIR] = jnp.concatenate(edges, axis=0).astype(BF16)


def adjoint(rest, masked, begun, select, lines, lags):
    devices, _, own = masked[0].shape
    depth = sum(part.shape[1] for part in masked)
    width = begun.shape[0]
    return call(
        functools.partial(adjoint_kernel, lags),
        [
            ((8, depth), F32),
            ((width, depth), BF16),
            ((devices // 2, width - PAIR, own), BF16),
            ((devices // 4 * PAIR, own), BF16),
        ],
        [rest, *masked, begun, select, lines],
        "v" * 6,
        [pltpu.VMEM((width, depth), F32), pltpu.VMEM((width, own), BF16)],
        flops=2 * width * depth * own * devices,
        moved=depth * own * devices,
        name="adjoint",
    )


def mine_kernel(spread_ref, top_ref, low_ref, own_ref, rims_ref):
    count = top_ref.shape[0] // 4
    hours = own_ref.shape[1]
    for i in range(count):
        edges = []
        for k in (i, i + count):
            term = terms(spread_ref, (top_ref, low_ref), 2 * k)
            own_ref[k] = term[:hours]
            edges.append(term[hours : hours + RIM])
        rims_ref[i * PAIR : (i + 1) * PAIR] = jnp.concatenate(edges, axis=0)


def mine_part(spread, masked):
    devices, _, own = masked[0].shape
    depth = sum(part.shape[1] for part in masked)
    width = spread.shape[0]
    return call(
        mine_kernel,
        [((devices // 2, width - PAIR, own), F32), ((devices // 4 * PAIR, own), F32)],
        [spread, *masked],
        "vvv",
        flops=width * depth * own * devices,
        moved=depth * own * devices,
        name="mine",
    )


def narrow_kernel(mism_ref, after_ref, out_ref):
    del after_ref
    rows, depth = out_ref.shape[1], mism_ref.shape[1]
    row, column = (lax.broadcasted_iota(jnp.int32, (rows, depth), i) for i in range(2))
    first = (column == row * (depth // rows)).astype(F32)
    narrow = lax.dot_general(
        mism_ref[...],
        first,
        (((1,), (1,)), ((), ())),
        precision=lax.Precision.HIGHEST,
        preferred_element_type=F32,
    )
    out_ref[...] = narrow[:1]


def narrow(mism, after, rows):
    outs = [((1, rows), F32)]
    return call(narrow_kernel, outs, [mism, after], "va", flops=BUSY, name="narrow")[0]


def gate_kernel(rows_ref, after_ref, out_ref):
    del after_ref
    out_ref[...] = rows_ref[...]


def gate(rows, after):
    outs = [(rows.shape, rows.dtype)]
    return call(gate_kernel, outs, [rows, after], "va", name="gate")[0]


def join_rims_kernel(own_ref, came_ref, out_ref):
    out_ref[...] = (own_ref[...] + came_ref[...].astype(F32)).astype(BF16)


def join_rims(own, came):
    return call(join_rims_kernel, [(own.shape, BF16)], [own, came], "vv", name="rims")[0]


def join_kernel(own_ref, came_ref, after_ref, main_ref):
    del after_ref
    half, hours, _ = own_ref.shape
    for i in range(half // 2):
        for j in range(2):
            k = i + j * (half // 2)
            main_ref[i, j * hours : (j + 1) * hours] = own_ref[k] + came_ref[k].astype(F32)


def join(own, came, after):
    half, hours, columns = own.shape
    outs = [((half // 2, 2 * hours, columns), F32)]
    return call(join_kernel, outs, [own, came, after], "vva", flops=BUSY, name="join")[0]


def with_rims(main_ref, rims_ref, i, j):
    hours = main_ref.shape[1] // 2
    inside = (lax.axis_index("hour") < lax.axis_size("hour") - 1).astype(F32)
    rims = rims_ref[i * PAIR : (i + 1) * PAIR].astype(F32) * inside
    at = (j + 1) * hours - RIM
    last = main_ref[i, at : at + RIM] + rims[j * RIM : (j + 1) * RIM]
    return jnp.concatenate([main_ref[i, j * hours : at], last], axis=0)


def shares_kernel(j, main_ref, rims_ref, after_ref, first_ref, *outs):
    del after_ref
    first_ref[...] = with_rims(main_ref, rims_ref, 0, j)
    for i, out in enumerate(outs):
        out[...] = with_rims(main_ref, rims_ref, i + 1, j).astype(BF16)


def shares(main, rims, j, after):
    count, both, columns = main.shape
    shape = (both // 2, columns)
    outs = [(shape, F32)] + [(shape, BF16)] * (count - 1)
    first, *parts = call(
        functools.partial(shares_kernel, j), outs, [main, rims, after], "vva", flops=BUSY, name="shares"
    )
    return first, parts


def outward_kernel(first_ref, *refs):
    *arrived, out_ref = refs
    total = first_ref[...]
    for piece in arrived:
        total += piece[...].astype(F32)
    out_ref[...] = total.astype(out_ref.dtype)


def outward(first, arrived, dtype):
    operands = [first, *arrived]
    outs = [(first.shape, dtype)]
    return call(outward_kernel, outs, operands, "v" * len(operands), name="outward")[0]


def per_device(flux, footprint, tile_mask, rec_hour, observed, obs_weight, site_count):
    hours, own = flux.shape
    rows, lags, cells = footprint.shape
    devices = cells // own
    far = devices // 2
    near = range(2, far, 2)

    low = flux.astype(BF16)
    end = edge(low)
    masks = masks_of(tile_mask, end)
    block = block_of(low, turn(end, 1), masks)
    far_block = swap(block, far)
    foot = footprint.reshape(rows * lags, cells)
    blocks = tile_mask.shape[0]
    head = blocks * 3 // 8
    top = prepare(foot, masks, block, devices, 0, head)
    first = window(block, far_block, top)
    parts = [swap(first, k) for k in near]
    bottom = prepare(foot, masks, first, devices, head, blocks - head)
    select, lines = choose(
        rec_hour.reshape(1, rows),
        observed.reshape(1, rows),
        obs_weight.reshape(1, rows),
        site_count,
        first,
        lags,
        hours,
    )
    rest = pack([first, *parts], lines, bottom)
    masked = (top, bottom)
    begun = score(rest, masked)
    mism, spread, other, other_rims = adjoint(
        swap(rest, 1), masked, begun, select, lines, lags
    )

    came_rims = swap(other_rims, 1)
    own_part, own_rims = mine_part(spread, masked)
    rims = join_rims(own_rims, came_rims)
    came = swap(gate(other, rims), 1)
    back = turn(rims, -1)
    main = join(own_part, came, rims)
    far_sum, parts = shares(main, back, 1, rims)
    middle = len(near) // 2
    order = [middle, *range(middle), *range(middle + 1, len(near))]
    passed = {i: swap(parts[i], near[i]) for i in order}
    passed = [passed[i] for i in range(len(near))]
    near_sum, others = shares(main, back, 0, parts[0])
    arrived = [swap(part, k) for part, k in zip(others, near)]
    mism = narrow(mism, far_sum, rows)
    relay = outward(far_sum, passed, BF16)
    total = outward(near_sum, arrived, F32)
    gradient = total + swap(relay, far).astype(F32)
    return (gradient, mism.reshape(rows))


def solution(mesh):
    placed = (
        P("hour", "rcpt"),
        P(("hour", "rcpt"), None, None),
        P(("hour", "rcpt"), None, None),
        P(("hour", "rcpt")),
        P(("hour", "rcpt")),
        P(("hour", "rcpt")),
        P(("hour", "rcpt")),
    )
    return jax.shard_map(
        per_device,
        mesh=mesh,
        in_specs=placed,
        out_specs=(P("hour", "rcpt"), P(("hour", "rcpt"))),
        check_vma=False,
    )
```
